128 devices in a mesh: region: 4 (over z_hi, core), tile: 32 (over x, z_lo, y).
Axes of the slice: x: 4, y: 4, z: 4 (z_hi: 2, z_lo: 2; z = z_hi * 2 + z_lo), core: 2. Of those that a mesh axis runs over, the one named last changes fastest.
Arguments:
- pts_coords: float32 [32768, 2, 256], P(('region', 'tile')), may hold values from 0 to 127
- pts_height: float32 [32768, 256], P(('region', 'tile')), may hold values from -7 to 7
- pts_weight: float32 [32768, 256], P(('region', 'tile')), may hold values from 0.25 to 4
- block_dest: int32 [32768, 1], P(('region', 'tile')), may hold values from 0 to 31; in each aligned block of 256 rows (0 to 255, 256 to 511, ...) at most 16 rows name the same one
- block_count: int32 [32768], P(('region', 'tile')), may hold values from 64 to 256
- ground_mask: int32 [32768, 256], P(('region', 'tile')), may hold values 0 or 1
- fixed_mask: int32 [4096, 512], P('tile', 'region'), may hold values 0 or 1
Outputs:
- terrain: float32 [4096, 512], P('tile', 'region')
- ground_weight: float32 [4096, 512], P('tile', 'region')
The draws below stay inside these ranges and needn't reach their ends.
Inputs may be any that keep to these rules, and one draw needn't show every extreme that they name: `block_dest`: among the 256 blocks of one device, no tile is named by more than 16 blocks, a bound that some block reaches.
All inputs are finite; a program needn't handle non-finite values. No bound on the sum of `ground_mask` or of `fixed_mask` on one device may be relied on, other than what follows from the above.
Results may differ from the reference program's by a relative error of at most 0.0003.
The reference program's roundings to bfloat16 on the way count: a program that leaves them out, or rounds other values in their place, can miss the bound.
Values sent between devices are 32-bit elements; how exact they have to be, the bound alone decides.
A program may use at most 64 MiB of HBM per device.

```python
import math
import jax
import jax.numpy as jnp
import numpy as np
from jax import lax

G = 128
PB = 16
NB_DEV = 256
P_SIZE = 256
SWEEPS = 8
CAP = 16
NB_TOTAL = 32768
NX = 4096
NY = 512
GP = 8
NXP = 256
N_REGION = 4
N_TILE = 32


def draw_pts_height(key, part):
    key = jax.random.fold_in(key, 11)
    key_mag, key_sign, key_owner, key_noise = jax.random.split(key, 4)
    regions = NB_TOTAL // (NB_DEV * N_TILE)
    owners = NB_TOTAL // NB_DEV
    magnitude = jax.random.uniform(key_mag, (regions,), jnp.float32, 2.5, 4.0)
    flips = jax.random.randint(key_sign, (regions,), 0, 2)
    region_offset = magnitude * (2.0 * flips.astype(jnp.float32) - 1.0)
    owner_offset = jax.random.uniform(key_owner, (owners,), jnp.float32, -1.0, 1.0)
    offset = jnp.repeat(region_offset, NB_DEV * N_TILE) + jnp.repeat(owner_offset, NB_DEV)
    noise = jnp.clip(jax.random.normal(key_noise, (NB_TOTAL, P_SIZE), jnp.float32), -2.0, 2.0)
    return (offset[:, None] + noise).astype(jnp.float32)


def touch_ends(array, stream_key, low, top_value):
    longest = array.shape.index(max(array.shape))
    spots = []
    for shift in (0, 1):
        where = [jax.random.randint(jax.random.fold_in(stream_key, axis), (), 0, length) for axis, length in enumerate(array.shape)]
        where[longest] = (where[longest] + shift) % array.shape[longest]
        spots.append(tuple(where))
    return array.at[spots[0]].set(low).at[spots[1]].set(top_value)


def shard_levels(stream_key, dims, shards, least, top_value):
    def one(dim, shards_of):
        draws = jax.random.uniform(jax.random.fold_in(jax.random.fold_in(stream_key, 6), dim), (shards_of,), jnp.float32, least / len(shards), top_value / len(shards))
        return jnp.repeat(jnp.exp(draws), dims[dim] // shards_of).reshape((-1,) + (1,) * (len(dims) - dim - 1))

    gain = one(*shards[0])
    for cut in shards[1:]:
        gain = gain * one(*cut)
    return gain


def assign_block(stream_key, own, number, rows, count, top, most, lean):
    sequence = jax.random.permutation(stream_key, count)
    crowded, usual = portions_of(count, rows * top, most, lean, True), portions_of(count, rows * top, most, lean, False)
    places = jnp.arange(count)

    def named(sizes, rotation):
        used = int((sizes > 0).sum())
        fixed = max(1, used // 4)
        moved = fixed + (places - fixed + rotation * (used - fixed)) % max(1, count - fixed)
        return jnp.zeros((count,), jnp.int32).at[sequence[jnp.where(places < fixed, places, moved)]].set(jnp.asarray(sizes, jnp.int32))

    sizes = jnp.where(number % 4 == 0, named(crowded, number // 4), named(usual, number - number // 4 - 1))
    mixed = jax.random.permutation(jax.random.fold_in(own, 3), count)
    giver, sink = mixed[0:count // 2 * 2:2], mixed[1:count // 2 * 2:2]
    slack = jnp.minimum(sizes[giver] - 1, most - sizes[sink]) // 2
    slack = jnp.where((giver == sequence[0]) | (sink == sequence[0]) | (sizes[sink] == 0), 0, jnp.maximum(slack, 0))
    moved = jax.random.randint(jax.random.fold_in(own, 4), (count // 2,), 0, 1 << 20) % (slack + 1)
    sizes = sizes.at[giver].add(-moved).at[sink].add(moved)
    members = jnp.searchsorted(jnp.cumsum(sizes), jnp.arange(rows * top), side="right").astype(jnp.int32)
    table = members.reshape(top, rows).T
    table = table[jax.random.permutation(jax.random.fold_in(own, 1), rows)]
    rotation = jax.random.randint(jax.random.fold_in(own, 2), (rows, 1), 0, top)
    return jnp.take_along_axis(table, (jnp.arange(top)[None, :] + rotation) % top, axis=1)


def portions_of(number_of, total, most, lean, full):
    portions = [(1 << 20) // math.isqrt(standing ** lean) + 1 for standing in range(1, number_of + 1)]
    largest = most if full else min(most, max(-(-total // number_of), total * portions[0] // sum(portions)))
    least = 1 if total - largest >= number_of - 1 else 0
    counts, spare = [largest] + [least] * (number_of - 1), total - largest - least * (number_of - 1)
    while spare > 0:
        free = [i for i in range(1, number_of) if counts[i] < largest] or [i for i in range(1, number_of) if counts[i] < most]
        whole, left = sum([portions[i] for i in free]), spare
        for i in free:
            more = min(most - counts[i], max(1, left * portions[i] // whole), spare)
            counts[i] = counts[i] + more
            spare = spare - more
    return np.array(counts)


def setup_inputs(seed: int = 0) -> dict:
    arg_keys = jax.random.split(jax.random.key(seed), 8)
    pts_coords = jnp.clip(127.0 * jax.random.uniform(arg_keys[0], (NB_TOTAL, 2, P_SIZE), jnp.float32) ** shard_levels(arg_keys[0], (NB_TOTAL, 2, P_SIZE), ((0, 128),), -0.2, 0.2), 0.0, 127.0)
    pts_height = draw_pts_height(jax.random.fold_in(arg_keys[7], 71), 0)
    pts_weight = jnp.clip(jnp.exp(math.log(4.0) - 2.7725887 * jax.random.uniform(arg_keys[2], (NB_TOTAL, P_SIZE), jnp.float32) ** shard_levels(arg_keys[2], (NB_TOTAL, P_SIZE), ((0, 128),), -0.2, 0.2)), 0.25, 4.0)
    block_dest_keys = jax.random.split(jax.random.fold_in(arg_keys[3], 1), NB_TOTAL // NB_DEV)
    block_dest_turns = jax.random.permutation(jax.random.fold_in(arg_keys[3], 3), NB_TOTAL // NB_DEV)
    block_dest = jax.vmap(lambda own, number: assign_block(jax.random.fold_in(arg_keys[3], 2), own, number, NB_DEV, N_TILE, 1, CAP, 2))(block_dest_keys, block_dest_turns).reshape((NB_TOTAL, 1))
    block_count = touch_ends(jax.random.randint(arg_keys[4], (NB_TOTAL,), P_SIZE // 4, P_SIZE + 1), jax.random.fold_in(arg_keys[4], 1), P_SIZE // 4, P_SIZE).astype(jnp.int32)
    ground_mask = touch_ends((jax.random.randint(arg_keys[5], (NB_TOTAL, P_SIZE), 0, 4) < 3).astype(jnp.int32), jax.random.fold_in(arg_keys[5], 1), 0, 1)
    fixed_mask = touch_ends((jax.random.randint(arg_keys[6], (NX, NY), 0, 8) < 1).astype(jnp.int32), jax.random.fold_in(arg_keys[6], 1), 0, 1)
    return dict(pts_coords=pts_coords, pts_height=pts_height, pts_weight=pts_weight, block_dest=block_dest, block_count=block_count, ground_mask=ground_mask, fixed_mask=fixed_mask)


stiffness = 1.0
relaxation = 0.5
base_slack = 0.3
slope_slack = 1.0
softness = 0.2


def tent_weights(coord, anchor):
    return jnp.maximum(0.0, 1.0 - jnp.abs(coord - anchor))


def rounded(values):
    return lax.optimization_barrier(values.astype(jnp.bfloat16)).astype(jnp.float32)


def stencil(padded):
    centre = padded[2:-2, 2:-2]
    nearest = padded[1:-3, 2:-2] + padded[3:-1, 2:-2] + padded[2:-2, 1:-3] + padded[2:-2, 3:-1]
    diagonal = padded[1:-3, 1:-3] + padded[1:-3, 3:-1] + padded[3:-1, 1:-3] + padded[3:-1, 3:-1]
    farther = padded[:-4, 2:-2] + padded[4:, 2:-2] + padded[2:-2, :-4] + padded[2:-2, 4:]
    return 20.0 * centre - 8.0 * nearest + 2.0 * diagonal + farther


def reference(pts_coords, pts_height, pts_weight, block_dest, block_count, ground_mask, fixed_mask):
    slots = jnp.arange(P_SIZE, dtype=jnp.int32)
    is_live = (slots[None, :] < block_count[:, None]) & (ground_mask == 1)
    weight = jnp.where(is_live, pts_weight, 0.0).astype(jnp.float32)
    lifted = weight * pts_height
    coord_x = pts_coords[:, 0, :]
    coord_y = pts_coords[:, 1, :]
    base_x = jnp.floor(coord_x)
    base_y = jnp.floor(coord_y)
    block_ids = jnp.arange(NB_TOTAL, dtype=jnp.int32)
    region_of = block_ids // (NB_DEV * N_TILE)
    row_start = block_dest[:, 0] * G
    col_start = region_of * G
    density = jnp.zeros((NX * NY,), jnp.float32)
    heights = jnp.zeros((NX * NY,), jnp.float32)
    for shift_x in (0, 1):
        for shift_y in (0, 1):
            anchor_x = base_x + shift_x
            anchor_y = base_y + shift_y
            tent_x = tent_weights(coord_x, anchor_x)
            tent_y = rounded(tent_weights(coord_y, anchor_y))
            left_w = rounded(weight * tent_x)
            left_h = rounded(lifted * tent_x)
            index_x = jnp.minimum(anchor_x.astype(jnp.int32), G - 1)
            index_y = jnp.minimum(anchor_y.astype(jnp.int32), G - 1)
            cell = (row_start[:, None] + index_x) * NY + col_start[:, None] + index_y
            cell = cell.reshape(-1).astype(jnp.int32)
            density = density + jax.ops.segment_sum((left_w * tent_y).reshape(-1), cell, NX * NY)
            heights = heights + jax.ops.segment_sum((left_h * tent_y).reshape(-1), cell, NX * NY)
    density = density.reshape(NX, NY)
    heights = heights.reshape(NX, NY)
    terrain = heights / (density + 1.0)
    for sweep_no in range(SWEEPS):
        padded = jnp.pad(terrain, 2)
        residue = heights - density * terrain - stiffness * stencil(padded)
        terrain = terrain + relaxation * residue / (density + 20.0 * stiffness)
    panels = terrain.reshape(NXP, PB, NY // PB, PB).sum(axis=(1, 3)) * (1.0 / (PB * PB))
    rows_x = jnp.arange(NXP, dtype=jnp.float32)
    reach_x = NXP / 4.0
    kernel_x = jnp.exp(-((rows_x[:, None] - rows_x[None, :]) ** 2) / (2.0 * reach_x * reach_x))
    rows_y = jnp.arange(GP, dtype=jnp.float32)
    reach_y = GP / 2.0
    kernel_y = jnp.exp(-((rows_y[:, None] - rows_y[None, :]) ** 2) / (2.0 * reach_y * reach_y))
    grouped = panels.reshape(NXP, N_REGION, GP)
    numer = jnp.einsum("ij,jrb,cb->irc", kernel_x, grouped, kernel_y, precision=lax.Precision.HIGHEST)
    denom = jnp.sum(kernel_x, axis=1)[:, None, None] * jnp.sum(kernel_y, axis=1)[None, None, :]
    trend = (numer / denom).reshape(NXP, N_REGION * GP)
    limit = base_slack + slope_slack * jnp.abs(panels - trend)
    limit = jnp.repeat(jnp.repeat(limit, PB, axis=0), PB, axis=1)
    limit = jnp.where(fixed_mask == 1, base_slack, limit)
    misfit = jnp.abs(heights - density * terrain) / (density + 1.0)
    ground_weight = jax.nn.sigmoid((limit - misfit) / softness)
    return terrain, ground_weight
```

```python
import functools

import jax
import jax.numpy as jnp
from jax import lax
from jax.experimental import pallas as pl
from jax.experimental.pallas import tpu as pltpu
from jax.sharding import PartitionSpec as P

MESH = pl.DeviceIdType.MESH
F32 = jnp.float32
BF16 = jnp.bfloat16

PB = 16
SWEEPS = 8
HALO = 2 * SWEEPS
CAP = 16
GROUP = 4

stiffness = 1.0
relaxation = 0.5
base_slack = 0.3
slope_slack = 1.0
softness = 0.2


def iota(shape, dim):
    return lax.broadcasted_iota(jnp.int32, shape, dim)


def tent(coord, anchor):
    return jnp.maximum(0.0, 1.0 - jnp.abs(coord - anchor))


def dot_exact(a, b):
    return jnp.dot(a, b, precision=lax.Precision.HIGHEST, preferred_element_type=F32)


def laplacian(v):
    rows, lanes = v.shape
    near = (
        pltpu.roll(v, 1, 0)
        + pltpu.roll(v, rows - 1, 0)
        + pltpu.roll(v, 1, 1)
        + pltpu.roll(v, lanes - 1, 1)
    )
    return near - 4.0 * v


def kernel(
    n_region,
    n_tile,
    coords_ref,
    height_ref,
    weight_ref,
    dest_ref,
    count_ref,
    ground_ref,
    fixed_ref,
    terrain_ref,
    soft_ref,
    payload,
    outbox,
    inbox,
    left_buf,
    right_buf,
    grids,
    edge,
    from_up,
    from_down,
    from_side,
    field,
    smooth,
    gathered,
    box_send,
    box_recv,
    halo_send,
    halo_recv,
    panel_send,
    panel_recv,
):
    region = lax.axis_index("region")
    tile = lax.axis_index("tile")
    blocks, points = height_ref.shape
    side = fixed_ref.shape[0]
    right = lax.rem(region + 1, n_region)
    left = lax.rem(region + n_region - 1, n_region)
    down = lax.rem(tile + 1, n_tile)
    up = lax.rem(tile + n_tile - 1, n_tile)

    barrier = pltpu.get_barrier_semaphore()

    def greet(shift, carry):
        pl.semaphore_signal(
            barrier, inc=1, device_id=(region, lax.rem(tile + shift, n_tile)), device_id_type=MESH
        )
        return carry

    lax.fori_loop(1, n_tile, greet, 0)
    for other in (left, right):
        for row in (up, tile, down):
            pl.semaphore_signal(barrier, inc=1, device_id=(other, row), device_id_type=MESH)

    eye = iota((blocks, blocks), 0) == iota((blocks, blocks), 1)
    dest_row = dest_ref[...].astype(F32)
    dest_col = jnp.sum(jnp.where(eye, dest_row, 0.0), axis=1, keepdims=True)
    count_col = jnp.sum(jnp.where(eye, count_ref[...].astype(F32), 0.0), axis=1, keepdims=True)
    live = (iota((blocks, points), 1).astype(F32) < count_col) & (ground_ref[...] == 1)
    weight = jnp.where(live, weight_ref[...], 0.0)
    values = (coords_ref[:, 0, :], coords_ref[:, 1, :], weight, weight * height_ref[...])
    for q, value in enumerate(values):
        for part in range(3):
            rounded = value.astype(BF16)
            payload[part * blocks : (part + 1) * blocks, q * points : (q + 1) * points] = rounded
            value = value - rounded.astype(F32)
    earlier = iota((blocks, blocks), 0) < iota((blocks, blocks), 1)
    order = jnp.sum(jnp.where((dest_col == dest_row) & earlier, 1.0, 0.0), axis=0, keepdims=True)
    away = dest_row - tile.astype(F32)
    away = jnp.where(away < 0.0, away + n_tile, away)
    slot_row = away * CAP + order

    pl.semaphore_wait(barrier, n_tile - 1 + 6)

    def box_copy(shift):
        return pltpu.make_async_remote_copy(
            src_ref=outbox.at[shift],
            dst_ref=inbox.at[shift],
            send_sem=box_send.at[shift],
            recv_sem=box_recv.at[shift],
            device_id=(region, lax.rem(tile + shift, n_tile)),
            device_id_type=MESH,
        )

    def pack(group, carry):
        rows = GROUP * CAP
        slots = iota((rows, blocks), 0) + group * rows
        pick = jnp.where(slots.astype(F32) == slot_row, 1.0, 0.0).astype(BF16)
        picked = jnp.dot(jnp.concatenate([pick] * 3, axis=1), payload[...], preferred_element_type=F32)
        first = pl.multiple_of(group * GROUP, GROUP)
        for q in range(4):
            piece = picked[:, q * points : (q + 1) * points].reshape(GROUP, CAP, points)
            outbox[pl.ds(first, GROUP), q * CAP : (q + 1) * CAP, :] = piece
        return carry

    def send_group(group, carry):
        pack(group, carry)

        def send(k, inner):
            @pl.when(group * GROUP + k > 0)
            def _():
                box_copy(group * GROUP + k).start()

            return inner

        return lax.fori_loop(0, GROUP, send, carry)

    lax.fori_loop(0, n_tile // GROUP, send_group, 0)

    inbox[0] = outbox[0]
    grids[...] = jnp.zeros_like(grids)
    anchors = iota((16, points), 0).astype(F32).astype(BF16)
    zero = jnp.zeros((16, points), BF16)

    def splat(shift, carry):
        @pl.when(shift > 0)
        def _():
            box_copy(shift).wait_recv()

        box = inbox[shift]
        x, y, w, u = [box[q * CAP : (q + 1) * CAP, :] for q in range(4)]
        x_low, y_low = jnp.floor(x), jnp.floor(y)
        x_high, y_high = x_low + 1.0, y_low + 1.0
        tx0, tx1 = tent(x, x_low), tent(x, x_high)
        rows = (x_low, x_high, y_low, y_high, w * tx0, w * tx1, u * tx0, u * tx1, tent(y, y_low), tent(y, y_high))
        for j in range(CAP):
            slot, col = (j // 4) % 2, (j % 4) * points
            spread = [jnp.broadcast_to(r[j : j + 1, :], (16, points)).astype(BF16) for r in rows]
            xl, xh, yl, yh, w0, w1, u0, u1, r0, r1 = spread
            for t in range(side // 16):
                at = anchors + BF16(16 * t)
                low, high = at == xl, at == xh
                lanes = slice(col, col + points)
                left_buf[slot, 16 * t : 16 * t + 16, lanes] = jnp.where(low, w0, jnp.where(high, w1, zero))
                left_buf[slot, side + 16 * t : side + 16 * t + 16, lanes] = jnp.where(
                    low, u0, jnp.where(high, u1, zero)
                )
                right_buf[slot, 16 * t : 16 * t + 16, lanes] = jnp.where(
                    at == yl, r0, jnp.where(at == yh, r1, zero)
                )
            if j % 4 == 3:
                grids[...] += lax.dot_general(
                    left_buf[slot], right_buf[slot], (((1,), (1,)), ((), ())), preferred_element_type=F32
                )
        return carry

    lax.fori_loop(0, n_tile, splat, 0)

    density, heights = grids[0:side, :], grids[side : 2 * side, :]
    lane = iota((side, side), 1)
    edge[...] = jnp.where(
        (lane < HALO) | (lane >= side - HALO),
        density,
        jnp.where(lane < 2 * HALO, pltpu.roll(heights, HALO, 1), pltpu.roll(heights, side - HALO, 1)),
    )

    def halo_copy(k, src, dst, device):
        return pltpu.make_async_remote_copy(
            src_ref=src,
            dst_ref=dst,
            send_sem=halo_send.at[k],
            recv_sem=halo_recv.at[k],
            device_id=device,
            device_id_type=MESH,
        )

    last = side - HALO
    copies = [
        halo_copy(0, edge, from_side.at[0], (left, tile)),
        halo_copy(1, edge, from_side.at[1], (right, tile)),
    ]
    for col, other in ((0, region), (1, left), (2, right)):
        for g in range(2):
            k = 2 + 4 * col + 2 * g
            copies.append(
                halo_copy(k, grids.at[pl.ds(g * side, HALO), :], from_down.at[col, g], (other, up))
            )
            copies.append(
                halo_copy(
                    k + 1, grids.at[pl.ds(g * side + last, HALO), :], from_up.at[col, g], (other, down)
                )
            )
    for copy in copies:
        copy.start()

    panels_side = side // PB
    all_panels = n_tile * panels_side
    reach_x = all_panels / 4.0
    reach_y = panels_side / 2.0
    own_row = iota((panels_side, all_panels), 0) + tile * panels_side
    slot = iota((panels_side, all_panels), 1)
    source = tile - slot // panels_side
    source = jnp.where(source < 0, source + n_tile, source)
    gap_x = (own_row - source * panels_side - slot % panels_side).astype(F32)
    kernel_x = jnp.exp(-(gap_x * gap_x) / (2.0 * reach_x * reach_x))
    cell_panel = iota((side, side), 0) // PB
    column = iota((side, side), 1)
    gap_y = (cell_panel - column).astype(F32)
    is_panel = column < panels_side
    area = 1.0 / (PB * PB)
    mean_of = jnp.where(is_panel & (cell_panel == column), area, 0.0)
    smooth_of = jnp.where(is_panel, jnp.exp(-(gap_y * gap_y) / (2.0 * reach_y * reach_y)) * area, 0.0)
    sum_y = jnp.sum(smooth_of, axis=0, keepdims=True) * (1.0 * PB)
    denom = jnp.sum(kernel_x, axis=1, keepdims=True) * jnp.where(iota((1, side), 1) < panels_side, sum_y, 1.0)
    spread_of = jnp.where(iota((side, side), 0) == iota((side, side), 1) // PB, 1.0, 0.0)

    for copy in copies:
        copy.wait()

    rows_all = side + 2 * HALO
    lane = iota((side, side), 1)
    strip = iota((HALO, side), 1)
    to_right, to_left = lane < HALO, lane >= side - HALO
    strip_right, strip_left = strip < HALO, strip >= side - HALO
    for g, (own, of_left, of_right) in enumerate(
        (
            (density, from_side[1], from_side[0]),
            (heights, pltpu.roll(from_side[1], HALO, 1), pltpu.roll(from_side[0], side - HALO, 1)),
        )
    ):
        field[g, HALO : HALO + side, 0:side] = own
        field[g, HALO : HALO + side, side : 2 * side] = jnp.where(
            to_right, of_right, jnp.where(to_left, of_left, 0.0)
        )
        for rows, got in ((slice(0, HALO), from_up), (slice(HALO + side, rows_all), from_down)):
            field[g, rows, 0:side] = got[0, g]
            field[g, rows, side : 2 * side] = jnp.where(
                strip_right, got[1, g], jnp.where(strip_left, got[2, g], 0.0)
            )

    row_at = iota((rows_all, 2 * side), 0) - HALO + tile * side
    lane_at = iota((rows_all, 2 * side), 1)
    col_at = jnp.where(lane_at < side + HALO, lane_at, lane_at - 2 * side) + region * side
    held = (lane_at < side + HALO) | (lane_at >= 2 * side - HALO)
    inside = held & (row_at >= 0) & (row_at < n_tile * side) & (col_at >= 0) & (col_at < n_region * side)
    dens, hts = field[0], field[1]
    field[2] = jnp.where(inside, relaxation / (dens + 20.0 * stiffness), 0.0)
    field[3] = jnp.where(inside, hts / (dens + 1.0), 0.0)

    def sweep(_, carry):
        v = field[3]
        residue = field[1] - field[0] * v - stiffness * laplacian(laplacian(v))
        field[3] = v + field[2] * residue
        return carry

    lax.fori_loop(0, SWEEPS, sweep, 0)
    terrain = field[3, HALO : HALO + side, 0:side]
    terrain_ref[...] = terrain

    sums = jnp.sum(terrain.reshape(panels_side, PB, side), axis=1)
    smooth[...] = dot_exact(sums, smooth_of)

    def panel_copy(shift):
        return pltpu.make_async_remote_copy(
            src_ref=smooth,
            dst_ref=gathered.at[shift],
            send_sem=panel_send.at[shift],
            recv_sem=panel_recv.at[shift],
            device_id=(region, lax.rem(tile + shift, n_tile)),
            device_id_type=MESH,
        )

    def send_panel(shift, carry):
        panel_copy(shift).start()
        return carry

    lax.fori_loop(1, n_tile, send_panel, 0)
    gathered[0] = smooth[...]
    panels = dot_exact(sums, mean_of)
    misfit = jnp.abs(grids[side : 2 * side, :] - grids[0:side, :] * terrain) / (grids[0:side, :] + 1.0)

    def wait_boxes(shift, carry):
        box_copy(shift).wait_send()
        return carry

    lax.fori_loop(1, n_tile, wait_boxes, 0)

    def wait_panel(shift, carry):
        panel_copy(shift).wait()
        return carry

    lax.fori_loop(1, n_tile, wait_panel, 0)
    numer = dot_exact(kernel_x, gathered[...].reshape(all_panels, side))
    limit = base_slack + slope_slack * jnp.abs(panels - numer / denom)
    limit = dot_exact(limit, spread_of)
    limit = jnp.broadcast_to(limit[:, None, :], (panels_side, PB, side)).reshape(side, side)
    limit = jnp.where(fixed_ref[...] == 1, base_slack, limit)
    soft_ref[...] = 1.0 / (1.0 + jnp.exp((misfit - limit) / softness))


def on_device(n_region, n_tile, pts_coords, pts_height, pts_weight, block_dest, block_count, ground_mask, fixed_mask):
    blocks, points = pts_height.shape
    side = fixed_mask.shape[0]
    rows_all = side + 2 * HALO
    panels_side = side // PB
    out = jax.ShapeDtypeStruct((side, side), F32)
    dma = pltpu.SemaphoreType.DMA
    return pl.pallas_call(
        functools.partial(kernel, n_region, n_tile),
        out_shape=(out, out),
        in_specs=[pl.BlockSpec(memory_space=pltpu.VMEM)] * 7,
        out_specs=[pl.BlockSpec(memory_space=pltpu.VMEM)] * 2,
        scratch_shapes=[
            pltpu.VMEM((3 * blocks, 4 * points), BF16),
            pltpu.VMEM((n_tile, 4 * CAP, points), F32),
            pltpu.VMEM((n_tile, 4 * CAP, points), F32),
            pltpu.VMEM((2, 2 * side, 4 * points), BF16),
            pltpu.VMEM((2, side, 4 * points), BF16),
            pltpu.VMEM((2 * side, side), F32),
            pltpu.VMEM((side, side), F32),
            pltpu.VMEM((3, 2, HALO, side), F32),
            pltpu.VMEM((3, 2, HALO, side), F32),
            pltpu.VMEM((2, side, side), F32),
            pltpu.VMEM((4, rows_all, 2 * side), F32),
            pltpu.VMEM((panels_side, side), F32),
            pltpu.VMEM((n_tile, panels_side, side), F32),
            dma((n_tile,)),
            dma((n_tile,)),
            dma((14,)),
            dma((14,)),
            dma((n_tile,)),
            dma((n_tile,)),
        ],
        compiler_params=pltpu.CompilerParams(
            collective_id=0, has_side_effects=True, vmem_limit_bytes=32 << 20
        ),
    )(
        pts_coords,
        pts_height,
        pts_weight,
        block_dest.reshape(1, blocks),
        block_count.reshape(1, blocks),
        ground_mask,
        fixed_mask,
    )


def solution(mesh):
    placed = (
        P(("region", "tile"), None, None),
        P(("region", "tile"), None),
        P(("region", "tile"), None),
        P(("region", "tile"), None),
        P(("region", "tile")),
        P(("region", "tile"), None),
        P("tile", "region"),
    )
    return jax.shard_map(
        functools.partial(on_device, mesh.shape["region"], mesh.shape["tile"]),
        mesh=mesh,
        in_specs=placed,
        out_specs=(P("tile", "region"), P("tile", "region")),
        check_vma=False,
    )
```

```python
import functools

import jax
import jax.numpy as jnp
from jax import lax
from jax.experimental import pallas as pl
from jax.experimental.pallas import tpu as pltpu
from jax.sharding import PartitionSpec as P

MESH = pl.DeviceIdType.MESH
F32 = jnp.float32
BF16 = jnp.bfloat16

PB = 16
SWEEPS = 8
HALO = 2 * SWEEPS
CAP = 16
GROUP = 8
WINDOW = 8

stiffness = 1.0
relaxation = 0.5
base_slack = 0.3
slope_slack = 1.0
softness = 0.2


def iota(shape, dim):
    return lax.broadcasted_iota(jnp.int32, shape, dim)


def tent(coord, anchor):
    return jnp.maximum(0.0, 1.0 - jnp.abs(coord - anchor))


def tile_step(tile, k, n_tile, sign):
    if n_tile != 32:
        return lax.rem(tile + sign * k + n_tile, n_tile)
    group, dx = k // 4, lax.rem(k, 4)
    dy = lax.rem(dx + group, 4)
    dz = lax.rem(dx + group + group // 4, 2)
    x, z, y = tile // 8, lax.rem(tile // 4, 2), lax.rem(tile, 4)
    x = lax.rem(x + sign * dx + 4, 4)
    y = lax.rem(y + sign * dy + 4, 4)
    z = lax.rem(z + dz, 2)
    return (x * 2 + z) * 4 + y


def order_of(dest, tile, n_tile):
    if n_tile != 32:
        return (dest - tile + n_tile) & (n_tile - 1)
    dx = ((dest >> 3) - tile // 8) & 3
    dz = ((dest >> 2) - tile // 4) & 1
    dy = (dest - tile) & 3
    low = (dy - dx) & 3
    high = (dz ^ dx ^ low) & 1
    return ((low + 4 * high) << 2) + dx


def dot_exact(a, b):
    return jnp.dot(a, b, precision=lax.Precision.HIGHEST, preferred_element_type=F32)


def laplacian(v):
    rows, lanes = v.shape
    near = (
        pltpu.roll(v, 1, 0)
        + pltpu.roll(v, rows - 1, 0)
        + pltpu.roll(v, 1, 1)
        + pltpu.roll(v, lanes - 1, 1)
    )
    return near - 4.0 * v


def kernel(
    n_region,
    n_tile,
    coords_hbm,
    height_hbm,
    weight_hbm,
    dest_hbm,
    count_hbm,
    ground_hbm,
    fixed_hbm,
    terrain_ref,
    soft_ref,
    coords_ref,
    height_ref,
    weight_ref,
    dest_ref,
    count_ref,
    ground_ref,
    fixed_ref,
    payload,
    outbox,
    inbox,
    left_buf,
    right_buf,
    grids,
    edge,
    from_up,
    from_down,
    from_side,
    field,
    smooth,
    gathered,
    box_send,
    box_recv,
    halo_send,
    halo_recv,
    panel_send,
    panel_recv,
    load_sem,
):
    region = lax.axis_index("region")
    tile = lax.axis_index("tile")
    blocks, points = height_hbm.shape
    side = fixed_hbm.shape[0]
    right = lax.rem(region + 1, n_region)
    left = lax.rem(region + n_region - 1, n_region)
    down = lax.rem(tile + 1, n_tile)
    up = lax.rem(tile + n_tile - 1, n_tile)

    loads = [
        pltpu.make_async_copy(src, dst, load_sem.at[i])
        for i, (src, dst) in enumerate(
            (
                (dest_hbm, dest_ref),
                (count_hbm, count_ref),
                (ground_hbm, ground_ref),
                (weight_hbm, weight_ref),
                (height_hbm, height_ref),
                (coords_hbm, coords_ref),
                (fixed_hbm, fixed_ref),
            )
        )
    ]
    for load in loads:
        load.start()

    barrier = pltpu.get_barrier_semaphore()

    def greet(shift, carry):
        pl.semaphore_signal(
            barrier, inc=1, device_id=(region, lax.rem(tile + shift, n_tile)), device_id_type=MESH
        )
        return carry

    lax.fori_loop(1, n_tile, greet, 0)
    for other in (left, right):
        for row in (up, tile, down):
            pl.semaphore_signal(barrier, inc=1, device_id=(other, row), device_id_type=MESH)

    for load in loads:
        load.wait()

    eye = iota((blocks, blocks), 0) == iota((blocks, blocks), 1)
    dest_row = dest_ref[...].astype(F32)
    dest_col = jnp.sum(jnp.where(eye, dest_row, 0.0), axis=1, keepdims=True)
    count_col = jnp.sum(jnp.where(eye, count_ref[...].astype(F32), 0.0), axis=1, keepdims=True)
    live = (iota((blocks, points), 1).astype(F32) < count_col) & (ground_ref[...] == 1)
    weight = jnp.where(live, weight_ref[...], 0.0)
    values = (coords_ref[:, 0, :], coords_ref[:, 1, :], weight, weight * height_ref[...])
    for q, value in enumerate(values):
        for part in range(3):
            rounded = value.astype(BF16)
            payload[part * blocks : (part + 1) * blocks, q * points : (q + 1) * points] = rounded
            value = value - rounded.astype(F32)
    earlier = iota((blocks, blocks), 0) < iota((blocks, blocks), 1)
    order = jnp.sum(jnp.where((dest_col == dest_row) & earlier, 1.0, 0.0), axis=0, keepdims=True)
    slot_row = order_of(dest_ref[...], tile, n_tile).astype(F32) * CAP + order

    pl.semaphore_wait(barrier, n_tile - 1 + 6)

    def box_copy(shift):
        return pltpu.make_async_remote_copy(
            src_ref=outbox.at[shift],
            dst_ref=inbox.at[shift],
            send_sem=box_send.at[shift],
            recv_sem=box_recv.at[shift],
            device_id=(region, tile_step(tile, shift, n_tile, 1)),
            device_id_type=MESH,
        )

    def pack(group, carry):
        rows = group_size * CAP
        slots = iota((rows, blocks), 0) + group * rows
        pick = jnp.where(slots.astype(F32) == slot_row, 1.0, 0.0).astype(BF16)
        picked = jnp.dot(jnp.concatenate([pick] * 3, axis=1), payload[...], preferred_element_type=F32)
        first = pl.multiple_of(group * group_size, group_size)
        for q in range(4):
            piece = picked[:, q * points : (q + 1) * points].reshape(group_size, CAP, points)
            outbox[pl.ds(first, group_size), q * CAP : (q + 1) * CAP, :] = piece
        return carry

    group_size = min(GROUP, n_tile)
    window = min(WINDOW, n_tile - 1)

    def send_group(group, carry):
        pack(group, carry)

        def send(k, inner):
            shift = group * group_size + k

            @pl.when((shift > 0) & (shift <= window))
            def _():
                box_copy(shift).start()

            return inner

        return lax.fori_loop(0, group_size, send, carry)

    lax.fori_loop(0, n_tile // group_size, send_group, 0)

    inbox[0] = outbox[0]
    grids[...] = jnp.zeros_like(grids)
    anchors = iota((16, points), 0).astype(F32).astype(BF16)
    zero = jnp.zeros((16, points), BF16)

    def splat(shift, carry):
        @pl.when(shift > 0)
        def _():
            box_copy(shift).wait_send()
            box_copy(shift).wait_recv()

        @pl.when((shift > 0) & (shift + window < n_tile))
        def _():
            box_copy(shift + window).start()

        box = inbox[shift]
        x, y, w, u = [box[q * CAP : (q + 1) * CAP, :] for q in range(4)]
        x_low, y_low = jnp.floor(x), jnp.floor(y)
        x_high, y_high = x_low + 1.0, y_low + 1.0
        tx0, tx1 = tent(x, x_low), tent(x, x_high)
        rows = (x_low, x_high, y_low, y_high, w * tx0, w * tx1, u * tx0, u * tx1, tent(y, y_low), tent(y, y_high))
        for j in range(CAP):
            slot, col = (j // 4) % 2, (j % 4) * points
            spread = [jnp.broadcast_to(r[j : j + 1, :], (16, points)).astype(BF16) for r in rows]
            xl, xh, yl, yh, w0, w1, u0, u1, r0, r1 = spread
            for t in range(side // 16):
                at = anchors + BF16(16 * t)
                low, high = at == xl, at == xh
                lanes = slice(col, col + points)
                left_buf[slot, 16 * t : 16 * t + 16, lanes] = jnp.where(low, w0, jnp.where(high, w1, zero))
                left_buf[slot, side + 16 * t : side + 16 * t + 16, lanes] = jnp.where(
                    low, u0, jnp.where(high, u1, zero)
                )
                right_buf[slot, 16 * t : 16 * t + 16, lanes] = jnp.where(
                    at == yl, r0, jnp.where(at == yh, r1, zero)
                )
            if j % 4 == 3:
                grids[...] += lax.dot_general(
                    left_buf[slot], right_buf[slot], (((1,), (1,)), ((), ())), preferred_element_type=F32
                )
        return carry

    lax.fori_loop(0, n_tile, splat, 0)

    density, heights = grids[0:side, :], grids[side : 2 * side, :]
    lane = iota((side, side), 1)
    edge[...] = jnp.where(
        (lane < HALO) | (lane >= side - HALO),
        density,
        jnp.where(lane < 2 * HALO, pltpu.roll(heights, HALO, 1), pltpu.roll(heights, side - HALO, 1)),
    )

    def halo_copy(k, src, dst, device):
        return pltpu.make_async_remote_copy(
            src_ref=src,
            dst_ref=dst,
            send_sem=halo_send.at[k],
            recv_sem=halo_recv.at[k],
            device_id=device,
            device_id_type=MESH,
        )

    last = side - HALO
    copies = [
        halo_copy(0, edge, from_side.at[0], (left, tile)),
        halo_copy(1, edge, from_side.at[1], (right, tile)),
    ]
    for col, other in ((0, region), (1, left), (2, right)):
        for g in range(2):
            k = 2 + 4 * col + 2 * g
            copies.append(
                halo_copy(k, grids.at[pl.ds(g * side, HALO), :], from_down.at[col, g], (other, up))
            )
            copies.append(
                halo_copy(
                    k + 1, grids.at[pl.ds(g * side + last, HALO), :], from_up.at[col, g], (other, down)
                )
            )
    for copy in copies:
        copy.start()

    panels_side = side // PB
    all_panels = n_tile * panels_side
    reach_x = all_panels / 4.0
    reach_y = panels_side / 2.0
    own_row = iota((panels_side, all_panels), 0) + tile * panels_side
    slot = iota((panels_side, all_panels), 1)
    source = tile - slot // panels_side
    source = jnp.where(source < 0, source + n_tile, source)
    gap_x = (own_row - source * panels_side - slot % panels_side).astype(F32)
    kernel_x = jnp.exp(-(gap_x * gap_x) / (2.0 * reach_x * reach_x))
    cell_panel = iota((side, side), 0) // PB
    column = iota((side, side), 1)
    gap_y = (cell_panel - column).astype(F32)
    is_panel = column < panels_side
    area = 1.0 / (PB * PB)
    mean_of = jnp.where(is_panel & (cell_panel == column), area, 0.0)
    smooth_of = jnp.where(is_panel, jnp.exp(-(gap_y * gap_y) / (2.0 * reach_y * reach_y)) * area, 0.0)
    sum_y = jnp.sum(smooth_of, axis=0, keepdims=True) * (1.0 * PB)
    denom = jnp.sum(kernel_x, axis=1, keepdims=True) * jnp.where(iota((1, side), 1) < panels_side, sum_y, 1.0)
    spread_of = jnp.where(iota((side, side), 0) == iota((side, side), 1) // PB, 1.0, 0.0)

    for copy in copies:
        copy.wait()

    rows_all = side + 2 * HALO
    lane = iota((side, side), 1)
    strip = iota((HALO, side), 1)
    to_right, to_left = lane < HALO, lane >= side - HALO
    strip_right, strip_left = strip < HALO, strip >= side - HALO
    for g, (own, of_left, of_right) in enumerate(
        (
            (density, from_side[1], from_side[0]),
            (heights, pltpu.roll(from_side[1], HALO, 1), pltpu.roll(from_side[0], side - HALO, 1)),
        )
    ):
        field[g, HALO : HALO + side, 0:side] = own
        field[g, HALO : HALO + side, side : 2 * side] = jnp.where(
            to_right, of_right, jnp.where(to_left, of_left, 0.0)
        )
        for rows, got in ((slice(0, HALO), from_up), (slice(HALO + side, rows_all), from_down)):
            field[g, rows, 0:side] = got[0, g]
            field[g, rows, side : 2 * side] = jnp.where(
                strip_right, got[1, g], jnp.where(strip_left, got[2, g], 0.0)
            )

    row_at = iota((rows_all, 2 * side), 0) - HALO + tile * side
    lane_at = iota((rows_all, 2 * side), 1)
    col_at = jnp.where(lane_at < side + HALO, lane_at, lane_at - 2 * side) + region * side
    held = (lane_at < side + HALO) | (lane_at >= 2 * side - HALO)
    inside = held & (row_at >= 0) & (row_at < n_tile * side) & (col_at >= 0) & (col_at < n_region * side)
    dens, hts = field[0], field[1]
    field[2] = jnp.where(inside, relaxation / (dens + 20.0 * stiffness), 0.0)
    field[3] = jnp.where(inside, hts / (dens + 1.0), 0.0)

    def sweep(_, carry):
        v = field[3]
        residue = field[1] - field[0] * v - stiffness * laplacian(laplacian(v))
        field[3] = v + field[2] * residue
        return carry

    lax.fori_loop(0, SWEEPS, sweep, 0)
    terrain = field[3, HALO : HALO + side, 0:side]
    terrain_ref[...] = terrain

    sums = jnp.sum(terrain.reshape(panels_side, PB, side), axis=1)
    smooth[...] = dot_exact(sums, smooth_of)

    def panel_copy(shift):
        return pltpu.make_async_remote_copy(
            src_ref=smooth,
            dst_ref=gathered.at[shift],
            send_sem=panel_send.at[shift],
            recv_sem=panel_recv.at[shift],
            device_id=(region, lax.rem(tile + shift, n_tile)),
            device_id_type=MESH,
        )

    def send_panel(shift, carry):
        panel_copy(shift).start()
        return carry

    lax.fori_loop(1, n_tile, send_panel, 0)
    gathered[0] = smooth[...]
    panels = dot_exact(sums, mean_of)
    misfit = jnp.abs(grids[side : 2 * side, :] - grids[0:side, :] * terrain) / (grids[0:side, :] + 1.0)

    def wait_panel(shift, carry):
        panel_copy(shift).wait()
        return carry

    lax.fori_loop(1, n_tile, wait_panel, 0)
    numer = dot_exact(kernel_x, gathered[...].reshape(all_panels, side))
    limit = base_slack + slope_slack * jnp.abs(panels - numer / denom)
    limit = dot_exact(limit, spread_of)
    limit = jnp.broadcast_to(limit[:, None, :], (panels_side, PB, side)).reshape(side, side)
    limit = jnp.where(fixed_ref[...] == 1, base_slack, limit)
    soft_ref[...] = 1.0 / (1.0 + jnp.exp((misfit - limit) / softness))


def on_device(n_region, n_tile, pts_coords, pts_height, pts_weight, block_dest, block_count, ground_mask, fixed_mask):
    blocks, points = pts_height.shape
    side = fixed_mask.shape[0]
    rows_all = side + 2 * HALO
    panels_side = side // PB
    out = jax.ShapeDtypeStruct((side, side), F32)
    dma = pltpu.SemaphoreType.DMA
    return pl.pallas_call(
        functools.partial(kernel, n_region, n_tile),
        out_shape=(out, out),
        in_specs=[pl.BlockSpec(memory_space=pltpu.HBM)] * 7,
        out_specs=[pl.BlockSpec(memory_space=pltpu.VMEM)] * 2,
        scratch_shapes=[
            pltpu.VMEM(pts_coords.shape, F32),
            pltpu.VMEM((blocks, points), F32),
            pltpu.VMEM((blocks, points), F32),
            pltpu.VMEM((1, blocks), jnp.int32),
            pltpu.VMEM((1, blocks), jnp.int32),
            pltpu.VMEM((blocks, points), jnp.int32),
            pltpu.VMEM((side, side), jnp.int32),
            pltpu.VMEM((3 * blocks, 4 * points), BF16),
            pltpu.VMEM((n_tile, 4 * CAP, points), F32),
            pltpu.VMEM((n_tile, 4 * CAP, points), F32),
            pltpu.VMEM((2, 2 * side, 4 * points), BF16),
            pltpu.VMEM((2, side, 4 * points), BF16),
            pltpu.VMEM((2 * side, side), F32),
            pltpu.VMEM((side, side), F32),
            pltpu.VMEM((3, 2, HALO, side), F32),
            pltpu.VMEM((3, 2, HALO, side), F32),
            pltpu.VMEM((2, side, side), F32),
            pltpu.VMEM((4, rows_all, 2 * side), F32),
            pltpu.VMEM((panels_side, side), F32),
            pltpu.VMEM((n_tile, panels_side, side), F32),
            dma((n_tile,)),
            dma((n_tile,)),
            dma((14,)),
            dma((14,)),
            dma((n_tile,)),
            dma((n_tile,)),
            dma((7,)),
        ],
        compiler_params=pltpu.CompilerParams(
            collective_id=0, has_side_effects=True, vmem_limit_bytes=32 << 20
        ),
    )(
        pts_coords,
        pts_height,
        pts_weight,
        block_dest.reshape(1, blocks),
        block_count.reshape(1, blocks),
        ground_mask,
        fixed_mask,
    )


def solution(mesh):
    placed = (
        P(("region", "tile"), None, None),
        P(("region", "tile"), None),
        P(("region", "tile"), None),
        P(("region", "tile"), None),
        P(("region", "tile")),
        P(("region", "tile"), None),
        P("tile", "region"),
    )
    return jax.shard_map(
        functools.partial(on_device, mesh.shape["region"], mesh.shape["tile"]),
        mesh=mesh,
        in_specs=placed,
        out_specs=(P("tile", "region"), P("tile", "region")),
        check_vma=False,
    )
```

```python
import functools

import jax
import jax.numpy as jnp
from jax import lax
from jax.experimental import pallas as pl
from jax.experimental.pallas import tpu as pltpu
from jax.sharding import PartitionSpec as P

MESH = pl.DeviceIdType.MESH
F32 = jnp.float32
BF16 = jnp.bfloat16

PB = 16
SWEEPS = 8
HALO = 2 * SWEEPS
CAP = 16
WINDOW = 14
PAD = 8
ROWS = 32

stiffness = 1.0
relaxation = 0.5
base_slack = 0.3
slope_slack = 1.0
softness = 0.2


def iota(shape, dim):
    return lax.broadcasted_iota(jnp.int32, shape, dim)


def tent(coord, anchor):
    return jnp.maximum(0.0, 1.0 - jnp.abs(coord - anchor))


def partner_order(n_tile):
    if n_tile != 32:
        return list(range(n_tile))
    load = [0] * 5
    left = set(range(1, 32))
    order = [0]
    while left:

        def after(step):
            dx, dz, dy = step // 8, step // 4 % 2, step % 4
            added = (dx in (1, 2), dx in (2, 3), dy in (1, 2), dy in (2, 3), dz)
            return [have + more for have, more in zip(load, added)]

        step = min(left, key=lambda c: (max(after(c)), sum(after(c)), sum(v * v for v in after(c)), c))
        load = after(step)
        left.remove(step)
        order.append(step)
    return order


def tile_step(tile, k, n_tile):
    order = partner_order(n_tile)
    step = order[0]
    for place in range(1, n_tile):
        step = jnp.where(k == place, order[place], step)
    if n_tile != 32:
        return lax.rem(tile + step, n_tile)
    x, z, y = tile // 8, lax.rem(tile // 4, 2), lax.rem(tile, 4)
    x = lax.rem(x + step // 8, 4)
    z = lax.rem(z + step // 4, 2)
    y = lax.rem(y + step, 4)
    return (x * 2 + z) * 4 + y


def order_of(dest, tile, n_tile):
    if n_tile != 32:
        return (dest - tile + n_tile) & (n_tile - 1)
    dx = ((dest >> 3) - tile // 8) & 3
    dz = ((dest >> 2) - tile // 4) & 1
    dy = (dest - tile) & 3
    step = dx * 8 + dz * 4 + dy
    place = jnp.zeros_like(step)
    for at, candidate in enumerate(partner_order(n_tile)):
        place = jnp.where(step == candidate, at, place)
    return place


def dot_exact(a, b):
    return jnp.dot(a, b, precision=lax.Precision.HIGHEST, preferred_element_type=F32)


def laplacian(cells, first):
    side = cells.shape[2]
    lane = iota((ROWS, side), 1)
    centre = [cells[k, PAD + first : PAD + first + ROWS, :] for k in range(2)]
    after = [pltpu.roll(c, 1, 1) for c in centre]
    before = [pltpu.roll(c, side - 1, 1) for c in centre]
    out = []
    for k in range(2):
        west = jnp.where(lane == 0, after[1 - k], after[k])
        east = jnp.where(lane == side - 1, before[1 - k], before[k])
        north = cells[k, PAD + first - 1 : PAD + first - 1 + ROWS, :]
        south = cells[k, PAD + first + 1 : PAD + first + 1 + ROWS, :]
        out.append((west + east) + (north + south) - 4.0 * centre[k])
    return out


def kernel(
    n_region,
    n_tile,
    coords_hbm,
    height_hbm,
    weight_hbm,
    dest_hbm,
    count_hbm,
    ground_hbm,
    fixed_hbm,
    terrain_ref,
    soft_ref,
    coords_ref,
    height_ref,
    weight_ref,
    dest_ref,
    count_ref,
    ground_ref,
    fixed_ref,
    payload,
    outbox,
    inbox,
    left_buf,
    right_buf,
    grids,
    edge,
    edge_turned,
    from_up,
    from_down,
    from_side,
    corner,
    field,
    cells,
    curved,
    smooth,
    gathered,
    box_send,
    box_recv,
    halo_send,
    halo_recv,
    panel_send,
    panel_recv,
    load_sem,
):
    region = lax.axis_index("region")
    tile = lax.axis_index("tile")
    blocks, points = height_hbm.shape
    side = fixed_hbm.shape[0]
    right = lax.rem(region + 1, n_region)
    left = lax.rem(region + n_region - 1, n_region)
    down = lax.rem(tile + 1, n_tile)
    up = lax.rem(tile + n_tile - 1, n_tile)

    loads = [
        pltpu.make_async_copy(src, dst, load_sem.at[i])
        for i, (src, dst) in enumerate(
            (
                (dest_hbm, dest_ref),
                (count_hbm, count_ref),
                (ground_hbm, ground_ref),
                (weight_hbm, weight_ref),
                (height_hbm, height_ref),
                (coords_hbm, coords_ref),
                (fixed_hbm, fixed_ref),
            )
        )
    ]
    for load in loads:
        load.start()

    barrier = pltpu.get_barrier_semaphore()

    def greet(shift, carry):
        pl.semaphore_signal(
            barrier, inc=1, device_id=(region, lax.rem(tile + shift, n_tile)), device_id_type=MESH
        )
        return carry

    lax.fori_loop(1, n_tile, greet, 0)
    for other in (left, right):
        for row in (up, tile, down):
            pl.semaphore_signal(barrier, inc=1, device_id=(other, row), device_id_type=MESH)

    for load in loads:
        load.wait()

    eye = iota((blocks, blocks), 0) == iota((blocks, blocks), 1)
    dest_row = dest_ref[...].astype(F32)
    dest_col = jnp.sum(jnp.where(eye, dest_row, 0.0), axis=1, keepdims=True)
    count_col = jnp.sum(jnp.where(eye, count_ref[...].astype(F32), 0.0), axis=1, keepdims=True)
    live = (iota((blocks, points), 1).astype(F32) < count_col) & (ground_ref[...] == 1)
    weight = jnp.where(live, weight_ref[...], 0.0)
    values = (coords_ref[:, 0, :], coords_ref[:, 1, :], weight, weight * height_ref[...])
    for q, value in enumerate(values):
        for part in range(3):
            rounded = value.astype(BF16)
            payload[part * blocks : (part + 1) * blocks, q * points : (q + 1) * points] = rounded
            value = value - rounded.astype(F32)
    earlier = iota((blocks, blocks), 0) < iota((blocks, blocks), 1)
    order = jnp.sum(jnp.where((dest_col == dest_row) & earlier, 1.0, 0.0), axis=0, keepdims=True)
    slot_row = order_of(dest_ref[...], tile, n_tile).astype(F32) * CAP + order

    def box_copy(shift):
        return pltpu.make_async_remote_copy(
            src_ref=outbox.at[shift],
            dst_ref=inbox.at[shift],
            send_sem=box_send.at[shift],
            recv_sem=box_recv.at[shift],
            device_id=(region, tile_step(tile, shift, n_tile)),
            device_id_type=MESH,
        )

    window = min(WINDOW, n_tile - 1)
    half = n_tile // 2
    for first in (0, half):
        slots = iota((half * CAP, blocks), 0) + first * CAP
        pick = jnp.where(slots.astype(F32) == slot_row, 1.0, 0.0).astype(BF16)
        pick = jnp.concatenate([pick] * 3, axis=1)
        for q in range(4):
            picked = jnp.dot(pick, payload[:, q * points : (q + 1) * points], preferred_element_type=F32)
            outbox[first : first + half, q * CAP : (q + 1) * CAP, :] = picked.reshape(half, CAP, points)
    pl.semaphore_wait(barrier, n_tile - 1 + 6)

    def send(shift, carry):
        box_copy(shift).start()
        return carry

    lax.fori_loop(1, window + 1, send, 0)

    inbox[0] = outbox[0]
    grids[...] = jnp.zeros_like(grids)
    anchors = iota((16, points), 0).astype(F32).astype(BF16)
    zero = jnp.zeros((16, points), BF16)

    def splat(shift, carry):
        @pl.when(shift > 0)
        def _():
            box_copy(shift).wait_send()
            box_copy(shift).wait_recv()

        @pl.when((shift > 0) & (shift + window < n_tile))
        def _():
            box_copy(shift + window).start()

        box = inbox[shift]
        x, y, w, u = [box[q * CAP : (q + 1) * CAP, :] for q in range(4)]
        x_low, y_low = jnp.floor(x), jnp.floor(y)
        x_high, y_high = x_low + 1.0, y_low + 1.0
        tx0, tx1 = tent(x, x_low), tent(x, x_high)
        rows = (x_low, x_high, y_low, y_high, w * tx0, w * tx1, u * tx0, u * tx1, tent(y, y_low), tent(y, y_high))
        for j in range(CAP):
            slot, col = (j // 4) % 2, (j % 4) * points
            spread = [jnp.broadcast_to(r[j : j + 1, :], (16, points)).astype(BF16) for r in rows]
            xl, xh, yl, yh, w0, w1, u0, u1, r0, r1 = spread
            for t in range(side // 16):
                at = anchors + BF16(16 * t)
                low, high = at == xl, at == xh
                lanes = slice(col, col + points)
                left_buf[slot, 16 * t : 16 * t + 16, lanes] = jnp.where(low, w0, jnp.where(high, w1, zero))
                left_buf[slot, side + 16 * t : side + 16 * t + 16, lanes] = jnp.where(
                    low, u0, jnp.where(high, u1, zero)
                )
                right_buf[slot, 16 * t : 16 * t + 16, lanes] = jnp.where(
                    at == yl, r0, jnp.where(at == yh, r1, zero)
                )
            if j % 4 == 3:
                grids[...] += lax.dot_general(
                    left_buf[slot], right_buf[slot], (((1,), (1,)), ((), ())), preferred_element_type=F32
                ).reshape(2, side, side)
        return carry

    lax.fori_loop(0, n_tile, splat, 0)

    density, heights = grids[0], grids[1]
    last = side - HALO
    lane = iota((side, side), 1)
    both = jnp.where(
        (lane < HALO) | (lane >= last),
        density,
        jnp.where(lane < 2 * HALO, pltpu.roll(heights, HALO, 1), pltpu.roll(heights, last, 1)),
    )
    edge[...] = both
    edge_turned[...] = both.T

    def halo_copy(k, src, dst, device):
        return pltpu.make_async_remote_copy(
            src_ref=src,
            dst_ref=dst,
            send_sem=halo_send.at[k],
            recv_sem=halo_recv.at[k],
            device_id=device,
            device_id_type=MESH,
        )

    head, tail = pl.ds(0, HALO), pl.ds(last, HALO)
    copies = [
        halo_copy(0, edge.at[head, :], corner.at[0], (left, up)),
        halo_copy(1, edge.at[head, :], corner.at[1], (right, up)),
        halo_copy(2, edge.at[tail, :], corner.at[2], (left, down)),
        halo_copy(3, edge.at[tail, :], corner.at[3], (right, down)),
        halo_copy(4, edge_turned.at[pl.ds(0, 2 * HALO), :], from_side.at[0], (left, tile)),
        halo_copy(5, edge_turned.at[pl.ds(side - 2 * HALO, 2 * HALO), :], from_side.at[1], (right, tile)),
        halo_copy(6, grids.at[:, head, :], from_down, (region, up)),
        halo_copy(7, grids.at[:, tail, :], from_up, (region, down)),
    ]
    for copy in copies:
        copy.start()

    panels_side = side // PB
    all_panels = n_tile * panels_side
    reach_x = all_panels / 4.0
    reach_y = panels_side / 2.0
    own_row = iota((panels_side, all_panels), 0) + tile * panels_side
    slot = iota((panels_side, all_panels), 1)
    source = tile - slot // panels_side
    source = jnp.where(source < 0, source + n_tile, source)
    gap_x = (own_row - source * panels_side - slot % panels_side).astype(F32)
    kernel_x = jnp.exp(-(gap_x * gap_x) / (2.0 * reach_x * reach_x))
    cell_panel = iota((side, side), 0) // PB
    column = iota((side, side), 1)
    gap_y = (cell_panel - column).astype(F32)
    is_panel = column < panels_side
    area = 1.0 / (PB * PB)
    mean_of = jnp.where(is_panel & (cell_panel == column), area, 0.0)
    smooth_of = jnp.where(is_panel, jnp.exp(-(gap_y * gap_y) / (2.0 * reach_y * reach_y)) * area, 0.0)
    sum_y = jnp.sum(smooth_of, axis=0, keepdims=True) * (1.0 * PB)
    denom = jnp.sum(kernel_x, axis=1, keepdims=True) * jnp.where(iota((1, side), 1) < panels_side, sum_y, 1.0)
    spread_of = jnp.where(iota((side, side), 0) == iota((side, side), 1) // PB, 1.0, 0.0)

    rows_all = side + 2 * HALO
    cells[...] = jnp.zeros_like(cells)
    curved[...] = jnp.zeros_like(curved)
    row_at = iota((rows_all, side), 0) - HALO + tile * side
    lane_at = iota((rows_all, side), 1)
    row_inside = (row_at >= 0) & (row_at < n_tile * side)
    side_inside = ((lane_at < HALO) & (region < n_region - 1)) | ((lane_at >= last) & (region > 0))
    insides = (row_inside, row_inside & side_inside)
    strip = iota((HALO, side), 1)
    middle = jnp.zeros((side - 2 * HALO, side), F32)

    for copy in copies:
        copy.wait()

    for g, own in enumerate((density, heights)):
        field[g, 0, HALO : HALO + side, :] = own
        field[g, 0, 0:HALO, :] = from_up[g]
        field[g, 0, HALO + side : rows_all, :] = from_down[g]
        of_right = from_side[0, g * HALO : (g + 1) * HALO, :]
        of_left = from_side[1, (1 - g) * HALO : (2 - g) * HALO, :]
        field[g, 1, HALO : HALO + side, :] = jnp.concatenate([of_right, middle, of_left], axis=0).T
        for rows, pair in ((slice(0, HALO), (2, 3)), (slice(HALO + side, rows_all), (0, 1))):
            of_right, of_left = corner[pair[0]], corner[pair[1]]
            if g == 1:
                of_right, of_left = pltpu.roll(of_right, last, 1), pltpu.roll(of_left, HALO, 1)
            field[g, 1, rows, :] = jnp.where(
                strip < HALO, of_right, jnp.where(strip >= last, of_left, 0.0)
            )
    for k, inside in enumerate(insides):
        dens, hts = field[0, k], field[1, k]
        field[2, k] = jnp.where(inside, relaxation / (dens + 20.0 * stiffness), 0.0)
        cells[k, PAD : PAD + rows_all, :] = jnp.where(inside, hts / (dens + 1.0), 0.0)

    def sweep(_, carry):
        for first in range(0, rows_all, ROWS):
            bent = laplacian(cells, first)
            for k in range(2):
                curved[k, PAD + first : PAD + first + ROWS, :] = bent[k]
        for first in range(0, rows_all, ROWS):
            bent = laplacian(curved, first)
            rows = slice(first, first + ROWS)
            for k in range(2):
                v = cells[k, PAD + first : PAD + first + ROWS, :]
                residue = field[1, k, rows, :] - field[0, k, rows, :] * v - stiffness * bent[k]
                cells[k, PAD + first : PAD + first + ROWS, :] = v + field[2, k, rows, :] * residue
        return carry

    lax.fori_loop(0, SWEEPS, sweep, 0)
    terrain = cells[0, PAD + HALO : PAD + HALO + side, :]
    terrain_ref[...] = terrain

    sums = jnp.sum(terrain.reshape(panels_side, PB, side), axis=1)
    smooth[...] = dot_exact(sums, smooth_of)

    def panel_copy(shift):
        return pltpu.make_async_remote_copy(
            src_ref=smooth,
            dst_ref=gathered.at[shift],
            send_sem=panel_send.at[shift],
            recv_sem=panel_recv.at[shift],
            device_id=(region, lax.rem(tile + shift, n_tile)),
            device_id_type=MESH,
        )

    def send_panel(shift, carry):
        panel_copy(shift).start()
        return carry

    lax.fori_loop(1, n_tile, send_panel, 0)
    gathered[0] = smooth[...]
    panels = dot_exact(sums, mean_of)
    misfit = jnp.abs(grids[1] - grids[0] * terrain) / (grids[0] + 1.0)

    def wait_panel(shift, carry):
        panel_copy(shift).wait()
        return carry

    lax.fori_loop(1, n_tile, wait_panel, 0)
    numer = dot_exact(kernel_x, gathered[...].reshape(all_panels, side))
    limit = base_slack + slope_slack * jnp.abs(panels - numer / denom)
    limit = dot_exact(limit, spread_of)
    limit = jnp.broadcast_to(limit[:, None, :], (panels_side, PB, side)).reshape(side, side)
    limit = jnp.where(fixed_ref[...] == 1, base_slack, limit)
    soft_ref[...] = 1.0 / (1.0 + jnp.exp((misfit - limit) / softness))


def on_device(n_region, n_tile, pts_coords, pts_height, pts_weight, block_dest, block_count, ground_mask, fixed_mask):
    blocks, points = pts_height.shape
    side = fixed_mask.shape[0]
    rows_all = side + 2 * HALO
    panels_side = side // PB
    out = jax.ShapeDtypeStruct((side, side), F32)
    dma = pltpu.SemaphoreType.DMA
    return pl.pallas_call(
        functools.partial(kernel, n_region, n_tile),
        out_shape=(out, out),
        in_specs=[pl.BlockSpec(memory_space=pltpu.HBM)] * 7,
        out_specs=[pl.BlockSpec(memory_space=pltpu.VMEM)] * 2,
        scratch_shapes=[
            pltpu.VMEM(pts_coords.shape, F32),
            pltpu.VMEM((blocks, points), F32),
            pltpu.VMEM((blocks, points), F32),
            pltpu.VMEM((1, blocks), jnp.int32),
            pltpu.VMEM((1, blocks), jnp.int32),
            pltpu.VMEM((blocks, points), jnp.int32),
            pltpu.VMEM((side, side), jnp.int32),
            pltpu.VMEM((3 * blocks, 4 * points), BF16),
            pltpu.VMEM((n_tile, 4 * CAP, points), F32),
            pltpu.VMEM((n_tile, 4 * CAP, points), F32),
            pltpu.VMEM((2, 2 * side, 4 * points), BF16),
            pltpu.VMEM((2, side, 4 * points), BF16),
            pltpu.VMEM((2, side, side), F32),
            pltpu.VMEM((side, side), F32),
            pltpu.VMEM((side, side), F32),
            pltpu.VMEM((2, HALO, side), F32),
            pltpu.VMEM((2, HALO, side), F32),
            pltpu.VMEM((2, 2 * HALO, side), F32),
            pltpu.VMEM((4, HALO, side), F32),
            pltpu.VMEM((3, 2, rows_all, side), F32),
            pltpu.VMEM((2, rows_all + 2 * PAD, side), F32),
            pltpu.VMEM((2, rows_all + 2 * PAD, side), F32),
            pltpu.VMEM((panels_side, side), F32),
            pltpu.VMEM((n_tile, panels_side, side), F32),
            dma((n_tile,)),
            dma((n_tile,)),
            dma((8,)),
            dma((8,)),
            dma((n_tile,)),
            dma((n_tile,)),
            dma((7,)),
        ],
        compiler_params=pltpu.CompilerParams(
            collective_id=0, has_side_effects=True, vmem_limit_bytes=60 << 20
        ),
    )(
        pts_coords,
        pts_height,
        pts_weight,
        block_dest.reshape(1, blocks),
        block_count.reshape(1, blocks),
        ground_mask,
        fixed_mask,
    )


def solution(mesh):
    placed = (
        P(("region", "tile"), None, None),
        P(("region", "tile"), None),
        P(("region", "tile"), None),
        P(("region", "tile"), None),
        P(("region", "tile")),
        P(("region", "tile"), None),
        P("tile", "region"),
    )
    return jax.shard_map(
        functools.partial(on_device, mesh.shape["region"], mesh.shape["tile"]),
        mesh=mesh,
        in_specs=placed,
        out_specs=(P("tile", "region"), P("tile", "region")),
        check_vma=False,
    )
```

```python
import functools

import jax
import jax.numpy as jnp
from jax import lax
from jax.experimental import pallas as pl
from jax.experimental.pallas import tpu as pltpu
from jax.sharding import PartitionSpec as P

MESH = pl.DeviceIdType.MESH
F32 = jnp.float32
BF16 = jnp.bfloat16

PB = 16
SWEEPS = 8
HALO = 2 * SWEEPS
CAP = 16
WINDOW = 12
GROUPS = 4
PAD = 8
ROWS = 32

stiffness = 1.0
relaxation = 0.5
base_slack = 0.3
slope_slack = 1.0
softness = 0.2


def iota(shape, dim):
    return lax.broadcasted_iota(jnp.int32, shape, dim)


def tent(coord, anchor):
    return jnp.maximum(0.0, 1.0 - jnp.abs(coord - anchor))


def partner_order(n_tile):
    if n_tile != 32:
        return list(range(n_tile))
    load = [0] * 5
    left = set(range(1, 32))
    order = [0]
    while left:

        def after(step):
            dx, dz, dy = step // 8, step // 4 % 2, step % 4
            added = (dx in (1, 2), dx in (2, 3), dy in (1, 2), dy in (2, 3), dz)
            return [have + more for have, more in zip(load, added)]

        step = min(left, key=lambda c: (max(after(c)), sum(after(c)), sum(v * v for v in after(c)), c))
        load = after(step)
        left.remove(step)
        order.append(step)
    return order


def tile_step(tile, k, n_tile):
    order = partner_order(n_tile)
    step = order[0]
    for place in range(1, n_tile):
        step = jnp.where(k == place, order[place], step)
    if n_tile != 32:
        return lax.rem(tile + step, n_tile)
    x, z, y = tile // 8, lax.rem(tile // 4, 2), lax.rem(tile, 4)
    x = lax.rem(x + step // 8, 4)
    z = lax.rem(z + step // 4, 2)
    y = lax.rem(y + step, 4)
    return (x * 2 + z) * 4 + y


def order_of(dest, tile, n_tile):
    if n_tile != 32:
        return (dest - tile + n_tile) & (n_tile - 1)
    dx = ((dest >> 3) - tile // 8) & 3
    dz = ((dest >> 2) - tile // 4) & 1
    dy = (dest - tile) & 3
    step = dx * 8 + dz * 4 + dy
    place = jnp.zeros_like(step)
    for at, candidate in enumerate(partner_order(n_tile)):
        place = jnp.where(step == candidate, at, place)
    return place


def dot_exact(a, b):
    return jnp.dot(a, b, precision=lax.Precision.HIGHEST, preferred_element_type=F32)


def laplacian(cells, first):
    side = cells.shape[2]
    lane = iota((ROWS, side), 1)
    centre = [cells[k, PAD + first : PAD + first + ROWS, :] for k in range(2)]
    after = [pltpu.roll(c, 1, 1) for c in centre]
    before = [pltpu.roll(c, side - 1, 1) for c in centre]
    out = []
    for k in range(2):
        west = jnp.where(lane == 0, after[1 - k], after[k])
        east = jnp.where(lane == side - 1, before[1 - k], before[k])
        north = cells[k, PAD + first - 1 : PAD + first - 1 + ROWS, :]
        south = cells[k, PAD + first + 1 : PAD + first + 1 + ROWS, :]
        out.append((west + east) + (north + south) - 4.0 * centre[k])
    return out


def kernel(
    n_region,
    n_tile,
    coords_hbm,
    height_hbm,
    weight_hbm,
    dest_hbm,
    count_hbm,
    ground_hbm,
    fixed_hbm,
    terrain_ref,
    soft_ref,
    coords_ref,
    height_ref,
    weight_ref,
    dest_ref,
    count_ref,
    ground_ref,
    fixed_ref,
    payload,
    outbox,
    inbox,
    left_buf,
    right_buf,
    grids,
    edge,
    edge_turned,
    from_up,
    from_down,
    from_side,
    corner,
    field,
    cells,
    curved,
    smooth,
    gathered,
    box_send,
    box_recv,
    halo_send,
    halo_recv,
    panel_send,
    panel_recv,
    load_sem,
):
    region = lax.axis_index("region")
    tile = lax.axis_index("tile")
    blocks, points = height_hbm.shape
    side = fixed_hbm.shape[0]
    right = lax.rem(region + 1, n_region)
    left = lax.rem(region + n_region - 1, n_region)
    down = lax.rem(tile + 1, n_tile)
    up = lax.rem(tile + n_tile - 1, n_tile)

    loads = [
        pltpu.make_async_copy(src, dst, load_sem.at[i])
        for i, (src, dst) in enumerate(
            (
                (dest_hbm, dest_ref),
                (count_hbm, count_ref),
                (ground_hbm, ground_ref),
                (weight_hbm, weight_ref),
                (height_hbm, height_ref),
                (coords_hbm, coords_ref),
                (fixed_hbm, fixed_ref),
            )
        )
    ]
    for load in loads:
        load.start()

    barrier = pltpu.get_barrier_semaphore()

    def greet(shift, carry):
        pl.semaphore_signal(
            barrier, inc=1, device_id=(region, lax.rem(tile + shift, n_tile)), device_id_type=MESH
        )
        return carry

    lax.fori_loop(1, n_tile, greet, 0)
    for other in (left, right):
        for row in (up, tile, down):
            pl.semaphore_signal(barrier, inc=1, device_id=(other, row), device_id_type=MESH)

    for load in loads[:2]:
        load.wait()
    eye = iota((blocks, blocks), 0) == iota((blocks, blocks), 1)
    dest_row = dest_ref[...].astype(F32)
    dest_col = jnp.sum(jnp.where(eye, dest_row, 0.0), axis=1, keepdims=True)
    count_col = jnp.sum(jnp.where(eye, count_ref[...].astype(F32), 0.0), axis=1, keepdims=True)
    earlier = iota((blocks, blocks), 0) < iota((blocks, blocks), 1)
    order = jnp.sum(jnp.where((dest_col == dest_row) & earlier, 1.0, 0.0), axis=0, keepdims=True)
    slot_row = order_of(dest_ref[...], tile, n_tile).astype(F32) * CAP + order

    def split(q, value):
        for part in range(3):
            rounded = value.astype(BF16)
            payload[part * blocks : (part + 1) * blocks, q * points : (q + 1) * points] = rounded
            value = value - rounded.astype(F32)

    for load in loads[2:4]:
        load.wait()
    live = (iota((blocks, points), 1).astype(F32) < count_col) & (ground_ref[...] == 1)
    weight = jnp.where(live, weight_ref[...], 0.0)
    split(2, weight)
    loads[4].wait()
    split(3, weight * height_ref[...])
    loads[5].wait()
    split(0, coords_ref[:, 0, :])
    split(1, coords_ref[:, 1, :])
    loads[6].wait()

    def box_copy(shift):
        return pltpu.make_async_remote_copy(
            src_ref=outbox.at[shift],
            dst_ref=inbox.at[shift],
            send_sem=box_send.at[shift],
            recv_sem=box_recv.at[shift],
            device_id=(region, tile_step(tile, shift, n_tile)),
            device_id_type=MESH,
        )

    window = min(WINDOW, n_tile - 1)
    group = n_tile // GROUPS
    for first in range(0, n_tile, group):
        slots = iota((group * CAP, blocks), 0) + first * CAP
        pick = jnp.where(slots.astype(F32) == slot_row, 1.0, 0.0).astype(BF16)
        pick = jnp.concatenate([pick] * 3, axis=1)
        for q in range(4):
            picked = jnp.dot(pick, payload[:, q * points : (q + 1) * points], preferred_element_type=F32)
            outbox[first : first + group, q * CAP : (q + 1) * CAP, :] = picked.reshape(group, CAP, points)
        if first == 0:
            pl.semaphore_wait(barrier, n_tile - 1 + 6)

        def send(shift, carry):
            box_copy(shift).start()
            return carry

        lax.fori_loop(max(first, 1), max(first, min(first + group, window + 1)), send, 0)

    inbox[0] = outbox[0]
    grids[...] = jnp.zeros_like(grids)
    anchors = iota((16, points), 0).astype(F32).astype(BF16)
    zero = jnp.zeros((16, points), BF16)

    def splat(shift, carry):
        @pl.when(shift > 0)
        def _():
            box_copy(shift).wait_send()

        @pl.when((shift > 0) & (shift + window < n_tile))
        def _():
            box_copy(shift + window).start()

        @pl.when(shift > 0)
        def _():
            box_copy(shift).wait_recv()

        box = inbox[shift]
        x, y, w, u = [box[q * CAP : (q + 1) * CAP, :] for q in range(4)]
        x_low, y_low = jnp.floor(x), jnp.floor(y)
        x_high, y_high = x_low + 1.0, y_low + 1.0
        tx0, tx1 = tent(x, x_low), tent(x, x_high)
        rows = (x_low, x_high, y_low, y_high, w * tx0, w * tx1, u * tx0, u * tx1, tent(y, y_low), tent(y, y_high))
        for j in range(CAP):
            slot, col = (j // 4) % 2, (j % 4) * points
            spread = [jnp.broadcast_to(r[j : j + 1, :], (16, points)).astype(BF16) for r in rows]
            xl, xh, yl, yh, w0, w1, u0, u1, r0, r1 = spread
            for t in range(side // 16):
                at = anchors + BF16(16 * t)
                low, high = at == xl, at == xh
                lanes = slice(col, col + points)
                left_buf[slot, 16 * t : 16 * t + 16, lanes] = jnp.where(low, w0, jnp.where(high, w1, zero))
                left_buf[slot, side + 16 * t : side + 16 * t + 16, lanes] = jnp.where(
                    low, u0, jnp.where(high, u1, zero)
                )
                right_buf[slot, 16 * t : 16 * t + 16, lanes] = jnp.where(
                    at == yl, r0, jnp.where(at == yh, r1, zero)
                )
            if j % 4 == 3:
                grids[...] += lax.dot_general(
                    left_buf[slot], right_buf[slot], (((1,), (1,)), ((), ())), preferred_element_type=F32
                ).reshape(2, side, side)
        return carry

    lax.fori_loop(0, n_tile, splat, 0)

    density, heights = grids[0], grids[1]
    last = side - HALO
    lane = iota((side, side), 1)
    both = jnp.where(
        (lane < HALO) | (lane >= last),
        density,
        jnp.where(lane < 2 * HALO, pltpu.roll(heights, HALO, 1), pltpu.roll(heights, last, 1)),
    )
    edge[...] = both
    edge_turned[...] = both.T

    def halo_copy(k, src, dst, device):
        return pltpu.make_async_remote_copy(
            src_ref=src,
            dst_ref=dst,
            send_sem=halo_send.at[k],
            recv_sem=halo_recv.at[k],
            device_id=device,
            device_id_type=MESH,
        )

    head, tail = pl.ds(0, HALO), pl.ds(last, HALO)
    copies = [
        halo_copy(0, edge.at[head, :], corner.at[0], (left, up)),
        halo_copy(1, edge.at[head, :], corner.at[1], (right, up)),
        halo_copy(2, edge.at[tail, :], corner.at[2], (left, down)),
        halo_copy(3, edge.at[tail, :], corner.at[3], (right, down)),
        halo_copy(4, edge_turned.at[pl.ds(0, 2 * HALO), :], from_side.at[0], (left, tile)),
        halo_copy(5, edge_turned.at[pl.ds(side - 2 * HALO, 2 * HALO), :], from_side.at[1], (right, tile)),
        halo_copy(6, grids.at[:, head, :], from_down, (region, up)),
        halo_copy(7, grids.at[:, tail, :], from_up, (region, down)),
    ]
    for copy in copies:
        copy.start()

    panels_side = side // PB
    all_panels = n_tile * panels_side
    reach_x = all_panels / 4.0
    reach_y = panels_side / 2.0
    own_row = iota((panels_side, all_panels), 0) + tile * panels_side
    slot = iota((panels_side, all_panels), 1)
    source = tile - slot // panels_side
    source = jnp.where(source < 0, source + n_tile, source)
    gap_x = (own_row - source * panels_side - slot % panels_side).astype(F32)
    kernel_x = jnp.exp(-(gap_x * gap_x) / (2.0 * reach_x * reach_x))
    gap_y = (iota((side, side), 0) // PB - iota((side, side), 1) // PB).astype(F32)
    area = 1.0 / (PB * PB)
    mean_of = jnp.where(gap_y == 0.0, area, 0.0)
    smooth_of = jnp.exp(-(gap_y * gap_y) / (2.0 * reach_y * reach_y)) * area
    sum_y = jnp.sum(smooth_of, axis=0, keepdims=True) * (1.0 * PB)
    inverse = 1.0 / (jnp.sum(kernel_x, axis=1, keepdims=True) * sum_y)

    rows_all = side + 2 * HALO
    cells[...] = jnp.zeros_like(cells)
    curved[...] = jnp.zeros_like(curved)
    row_at = iota((rows_all, side), 0) - HALO + tile * side
    lane_at = iota((rows_all, side), 1)
    row_inside = (row_at >= 0) & (row_at < n_tile * side)
    side_inside = ((lane_at < HALO) & (region < n_region - 1)) | ((lane_at >= last) & (region > 0))
    insides = (row_inside, row_inside & side_inside)
    strip = iota((HALO, side), 1)
    middle = jnp.zeros((side - 2 * HALO, side), F32)

    for copy in copies:
        copy.wait()

    for g, own in enumerate((density, heights)):
        field[g, 0, HALO : HALO + side, :] = own
        field[g, 0, 0:HALO, :] = from_up[g]
        field[g, 0, HALO + side : rows_all, :] = from_down[g]
        of_right = from_side[0, g * HALO : (g + 1) * HALO, :]
        of_left = from_side[1, (1 - g) * HALO : (2 - g) * HALO, :]
        field[g, 1, HALO : HALO + side, :] = jnp.concatenate([of_right, middle, of_left], axis=0).T
        for rows, pair in ((slice(0, HALO), (2, 3)), (slice(HALO + side, rows_all), (0, 1))):
            of_right, of_left = corner[pair[0]], corner[pair[1]]
            if g == 1:
                of_right, of_left = pltpu.roll(of_right, last, 1), pltpu.roll(of_left, HALO, 1)
            field[g, 1, rows, :] = jnp.where(
                strip < HALO, of_right, jnp.where(strip >= last, of_left, 0.0)
            )
    for k, inside in enumerate(insides):
        dens, hts = field[0, k], field[1, k]
        field[2, k] = jnp.where(inside, relaxation / (dens + 20.0 * stiffness), 0.0)
        cells[k, PAD : PAD + rows_all, :] = jnp.where(inside, hts / (dens + 1.0), 0.0)

    def sweep(_, carry):
        for first in range(0, rows_all, ROWS):
            bent = laplacian(cells, first)
            for k in range(2):
                curved[k, PAD + first : PAD + first + ROWS, :] = bent[k]
        for first in range(0, rows_all, ROWS):
            bent = laplacian(curved, first)
            rows = slice(first, first + ROWS)
            for k in range(2):
                v = cells[k, PAD + first : PAD + first + ROWS, :]
                residue = field[1, k, rows, :] - field[0, k, rows, :] * v - stiffness * bent[k]
                cells[k, PAD + first : PAD + first + ROWS, :] = v + field[2, k, rows, :] * residue
        return carry

    lax.fori_loop(0, SWEEPS, sweep, 0)
    terrain = cells[0, PAD + HALO : PAD + HALO + side, :]
    terrain_ref[...] = terrain

    sums = jnp.sum(terrain.reshape(panels_side, PB, side), axis=1)
    smooth[...] = dot_exact(sums, smooth_of)

    def panel_copy(shift):
        return pltpu.make_async_remote_copy(
            src_ref=smooth,
            dst_ref=gathered.at[shift],
            send_sem=panel_send.at[shift],
            recv_sem=panel_recv.at[shift],
            device_id=(region, lax.rem(tile + shift, n_tile)),
            device_id_type=MESH,
        )

    def send_panel(place, carry):
        panel_copy(lax.rem(place + n_tile // 2 - 1, n_tile - 1) + 1).start()
        return carry

    lax.fori_loop(0, n_tile - 1, send_panel, 0)
    gathered[0] = smooth[...]
    panels = dot_exact(sums, mean_of)
    misfit = jnp.abs(grids[1] - grids[0] * terrain) / (grids[0] + 1.0)

    def wait_panel(shift, carry):
        panel_copy(shift).wait()
        return carry

    lax.fori_loop(1, n_tile, wait_panel, 0)
    numer = dot_exact(kernel_x, gathered[...].reshape(all_panels, side))
    limit = base_slack + slope_slack * jnp.abs(panels - numer * inverse)
    limit = jnp.broadcast_to(limit[:, None, :], (panels_side, PB, side)).reshape(side, side)
    limit = jnp.where(fixed_ref[...] == 1, base_slack, limit)
    soft_ref[...] = 1.0 / (1.0 + jnp.exp((misfit - limit) / softness))


def on_device(n_region, n_tile, pts_coords, pts_height, pts_weight, block_dest, block_count, ground_mask, fixed_mask):
    blocks, points = pts_height.shape
    side = fixed_mask.shape[0]
    rows_all = side + 2 * HALO
    panels_side = side // PB
    out = jax.ShapeDtypeStruct((side, side), F32)
    dma = pltpu.SemaphoreType.DMA
    return pl.pallas_call(
        functools.partial(kernel, n_region, n_tile),
        out_shape=(out, out),
        in_specs=[pl.BlockSpec(memory_space=pltpu.HBM)] * 7,
        out_specs=[pl.BlockSpec(memory_space=pltpu.VMEM)] * 2,
        scratch_shapes=[
            pltpu.VMEM(pts_coords.shape, F32),
            pltpu.VMEM((blocks, points), F32),
            pltpu.VMEM((blocks, points), F32),
            pltpu.VMEM((1, blocks), jnp.int32),
            pltpu.VMEM((1, blocks), jnp.int32),
            pltpu.VMEM((blocks, points), jnp.int32),
            pltpu.VMEM((side, side), jnp.int32),
            pltpu.VMEM((3 * blocks, 4 * points), BF16),
            pltpu.VMEM((n_tile, 4 * CAP, points), F32),
            pltpu.VMEM((n_tile, 4 * CAP, points), F32),
            pltpu.VMEM((2, 2 * side, 4 * points), BF16),
            pltpu.VMEM((2, side, 4 * points), BF16),
            pltpu.VMEM((2, side, side), F32),
            pltpu.VMEM((side, side), F32),
            pltpu.VMEM((side, side), F32),
            pltpu.VMEM((2, HALO, side), F32),
            pltpu.VMEM((2, HALO, side), F32),
            pltpu.VMEM((2, 2 * HALO, side), F32),
            pltpu.VMEM((4, HALO, side), F32),
            pltpu.VMEM((3, 2, rows_all, side), F32),
            pltpu.VMEM((2, rows_all + 2 * PAD, side), F32),
            pltpu.VMEM((2, rows_all + 2 * PAD, side), F32),
            pltpu.VMEM((panels_side, side), F32),
            pltpu.VMEM((n_tile, panels_side, side), F32),
            dma((n_tile,)),
            dma((n_tile,)),
            dma((8,)),
            dma((8,)),
            dma((n_tile,)),
            dma((n_tile,)),
            dma((7,)),
        ],
        compiler_params=pltpu.CompilerParams(
            collective_id=0, has_side_effects=True, vmem_limit_bytes=40 << 20
        ),
    )(
        *[
            pltpu.with_memory_space_constraint(operand, pltpu.HBM)
            for operand in (
                pts_coords,
                pts_height,
                pts_weight,
                block_dest.reshape(1, blocks),
                block_count.reshape(1, blocks),
                ground_mask,
                fixed_mask,
            )
        ]
    )


def solution(mesh):
    placed = (
        P(("region", "tile"), None, None),
        P(("region", "tile"), None),
        P(("region", "tile"), None),
        P(("region", "tile"), None),
        P(("region", "tile")),
        P(("region", "tile"), None),
        P("tile", "region"),
    )
    return jax.shard_map(
        functools.partial(on_device, mesh.shape["region"], mesh.shape["tile"]),
        mesh=mesh,
        in_specs=placed,
        out_specs=(P("tile", "region"), P("tile", "region")),
        check_vma=False,
    )
```

```python
import functools

import jax
import jax.numpy as jnp
from jax import lax
from jax.experimental import pallas as pl
from jax.experimental.pallas import tpu as pltpu
from jax.sharding import PartitionSpec as P

MESH = pl.DeviceIdType.MESH
F32 = jnp.float32
BF16 = jnp.bfloat16

PB = 16
SWEEPS = 8
HALO = 2 * SWEEPS
CAP = 16
WINDOW = 18
GROUPS = 4
PAD = 8
ROWS = 32

stiffness = 1.0
relaxation = 0.5
base_slack = 0.3
slope_slack = 1.0
softness = 0.2


def iota(shape, dim):
    return lax.broadcasted_iota(jnp.int32, shape, dim)


def tent(coord, anchor):
    return jnp.maximum(0.0, 1.0 - jnp.abs(coord - anchor))


def partner_order(n_tile):
    if n_tile != 32:
        return list(range(n_tile))
    load = [0] * 5
    left = set(range(1, 32))
    order = [0]
    while left:

        def after(step):
            dx, dz, dy = step // 8, step // 4 % 2, step % 4
            added = (dx in (1, 2), dx in (2, 3), dy in (1, 2), dy in (2, 3), dz)
            return [have + more for have, more in zip(load, added)]

        step = min(left, key=lambda c: (max(after(c)), sum(after(c)), sum(v * v for v in after(c)), c))
        load = after(step)
        left.remove(step)
        order.append(step)
    return order


def tile_step(tile, k, n_tile):
    order = partner_order(n_tile)
    step = order[0]
    for place in range(1, n_tile):
        step = jnp.where(k == place, order[place], step)
    if n_tile != 32:
        return lax.rem(tile + step, n_tile)
    x, z, y = tile // 8, lax.rem(tile // 4, 2), lax.rem(tile, 4)
    x = lax.rem(x + step // 8, 4)
    z = lax.rem(z + step // 4, 2)
    y = lax.rem(y + step, 4)
    return (x * 2 + z) * 4 + y


def order_of(dest, tile, n_tile):
    if n_tile != 32:
        return (dest - tile + n_tile) & (n_tile - 1)
    dx = ((dest >> 3) - tile // 8) & 3
    dz = ((dest >> 2) - tile // 4) & 1
    dy = (dest - tile) & 3
    step = dx * 8 + dz * 4 + dy
    place = jnp.zeros_like(step)
    for at, candidate in enumerate(partner_order(n_tile)):
        place = jnp.where(step == candidate, at, place)
    return place


def dot_exact(a, b):
    return jnp.dot(a, b, precision=lax.Precision.HIGHEST, preferred_element_type=F32)


def laplacian(cells, first):
    side = cells.shape[2]
    lane = iota((ROWS, side), 1)
    centre = [cells[k, PAD + first : PAD + first + ROWS, :] for k in range(2)]
    after = [pltpu.roll(c, 1, 1) for c in centre]
    before = [pltpu.roll(c, side - 1, 1) for c in centre]
    out = []
    for k in range(2):
        west = jnp.where(lane == 0, after[1 - k], after[k])
        east = jnp.where(lane == side - 1, before[1 - k], before[k])
        north = cells[k, PAD + first - 1 : PAD + first - 1 + ROWS, :]
        south = cells[k, PAD + first + 1 : PAD + first + 1 + ROWS, :]
        out.append((west + east) + (north + south) - 4.0 * centre[k])
    return out


def kernel(
    n_region,
    n_tile,
    coords_hbm,
    height_hbm,
    weight_hbm,
    dest_hbm,
    count_hbm,
    ground_hbm,
    fixed_hbm,
    terrain_ref,
    soft_ref,
    coords_ref,
    height_ref,
    weight_ref,
    dest_ref,
    count_ref,
    ground_ref,
    fixed_ref,
    payload,
    outbox,
    inbox,
    left_buf,
    right_buf,
    grids,
    edge,
    edge_turned,
    from_up,
    from_down,
    from_side,
    corner,
    field,
    cells,
    curved,
    smooth,
    gathered,
    box_send,
    box_recv,
    halo_send,
    halo_recv,
    panel_send,
    panel_recv,
    load_sem,
):
    region = lax.axis_index("region")
    tile = lax.axis_index("tile")
    blocks, points = height_hbm.shape
    side = fixed_hbm.shape[0]
    right = lax.rem(region + 1, n_region)
    left = lax.rem(region + n_region - 1, n_region)
    down = lax.rem(tile + 1, n_tile)
    up = lax.rem(tile + n_tile - 1, n_tile)

    loads = [
        pltpu.make_async_copy(src, dst, load_sem.at[i])
        for i, (src, dst) in enumerate(
            (
                (dest_hbm, dest_ref),
                (count_hbm, count_ref),
                (ground_hbm, ground_ref),
                (weight_hbm, weight_ref),
                (height_hbm, height_ref),
                (coords_hbm.at[:, 0, :], coords_ref.at[0]),
                (coords_hbm.at[:, 1, :], coords_ref.at[1]),
                (fixed_hbm, fixed_ref),
            )
        )
    ]
    for load in loads:
        load.start()

    barrier = pltpu.get_barrier_semaphore()

    def greet(shift, carry):
        pl.semaphore_signal(
            barrier, inc=1, device_id=(region, lax.rem(tile + shift, n_tile)), device_id_type=MESH
        )
        return carry

    lax.fori_loop(1, n_tile, greet, 0)
    for other in (left, right):
        for row in (up, tile, down):
            pl.semaphore_signal(barrier, inc=1, device_id=(other, row), device_id_type=MESH)

    for load in loads[:2]:
        load.wait()
    eye = iota((blocks, blocks), 0) == iota((blocks, blocks), 1)
    dest_row = dest_ref[...].astype(F32)
    dest_col = jnp.sum(jnp.where(eye, dest_row, 0.0), axis=1, keepdims=True)
    count_col = jnp.sum(jnp.where(eye, count_ref[...].astype(F32), 0.0), axis=1, keepdims=True)
    earlier = iota((blocks, blocks), 0) < iota((blocks, blocks), 1)
    order = jnp.sum(jnp.where((dest_col == dest_row) & earlier, 1.0, 0.0), axis=0, keepdims=True)
    slot_row = order_of(dest_ref[...], tile, n_tile).astype(F32) * CAP + order

    def split(q, value):
        for part in range(3):
            rounded = value.astype(BF16)
            payload[part * blocks : (part + 1) * blocks, q * points : (q + 1) * points] = rounded
            value = value - rounded.astype(F32)

    for load in loads[2:4]:
        load.wait()
    live = (iota((blocks, points), 1).astype(F32) < count_col) & (ground_ref[...] == 1)
    weight = jnp.where(live, weight_ref[...], 0.0)
    split(2, weight)
    loads[4].wait()
    split(3, weight * height_ref[...])
    loads[5].wait()
    split(0, coords_ref[0])
    loads[6].wait()
    split(1, coords_ref[1])
    loads[7].wait()

    def box_copy(shift):
        return pltpu.make_async_remote_copy(
            src_ref=outbox.at[shift],
            dst_ref=inbox.at[shift],
            send_sem=box_send.at[shift],
            recv_sem=box_recv.at[shift],
            device_id=(region, tile_step(tile, shift, n_tile)),
            device_id_type=MESH,
        )

    window = min(WINDOW, n_tile - 1)
    group = n_tile // GROUPS
    for first in range(0, n_tile, group):
        slots = iota((group * CAP, blocks), 0) + first * CAP
        pick = jnp.where(slots.astype(F32) == slot_row, 1.0, 0.0).astype(BF16)
        pick = jnp.concatenate([pick] * 3, axis=1)
        for q in range(4):
            picked = jnp.dot(pick, payload[:, q * points : (q + 1) * points], preferred_element_type=F32)
            outbox[first : first + group, q * CAP : (q + 1) * CAP, :] = picked.reshape(group, CAP, points)
        if first == 0:
            pl.semaphore_wait(barrier, n_tile - 1 + 6)

        def send(shift, carry):
            box_copy(shift).start()
            return carry

        lax.fori_loop(max(first, 1), max(first, min(first + group, window + 1)), send, 0)

    inbox[0] = outbox[0]
    grids[...] = jnp.zeros_like(grids)
    anchors = iota((16, points), 0).astype(F32).astype(BF16)
    zero = jnp.zeros((16, points), BF16)

    def splat(shift, carry):
        @pl.when(shift > 0)
        def _():
            box_copy(shift).wait_send()

        @pl.when((shift > 0) & (shift + window < n_tile))
        def _():
            box_copy(shift + window).start()

        @pl.when(shift > 0)
        def _():
            box_copy(shift).wait_recv()

        box = inbox[shift]
        x, y, w, u = [box[q * CAP : (q + 1) * CAP, :] for q in range(4)]
        x_low, y_low = jnp.floor(x), jnp.floor(y)
        x_high, y_high = x_low + 1.0, y_low + 1.0
        tx0, tx1 = tent(x, x_low), tent(x, x_high)
        rows = (x_low, x_high, y_low, y_high, w * tx0, w * tx1, u * tx0, u * tx1, tent(y, y_low), tent(y, y_high))
        for j in range(CAP):
            slot, col = (j // 4) % 2, (j % 4) * points
            spread = [jnp.broadcast_to(r[j : j + 1, :], (16, points)).astype(BF16) for r in rows]
            xl, xh, yl, yh, w0, w1, u0, u1, r0, r1 = spread
            for t in range(side // 16):
                at = anchors + BF16(16 * t)
                low, high = at == xl, at == xh
                lanes = slice(col, col + points)
                left_buf[slot, 16 * t : 16 * t + 16, lanes] = jnp.where(low, w0, jnp.where(high, w1, zero))
                left_buf[slot, side + 16 * t : side + 16 * t + 16, lanes] = jnp.where(
                    low, u0, jnp.where(high, u1, zero)
                )
                right_buf[slot, 16 * t : 16 * t + 16, lanes] = jnp.where(
                    at == yl, r0, jnp.where(at == yh, r1, zero)
                )
            if j % 4 == 3:
                grids[...] += lax.dot_general(
                    left_buf[slot], right_buf[slot], (((1,), (1,)), ((), ())), preferred_element_type=F32
                ).reshape(2, side, side)
        return carry

    lax.fori_loop(0, n_tile, splat, 0)

    last = side - HALO
    head, tail = pl.ds(0, HALO), pl.ds(last, HALO)

    def halo_copy(k, src, dst, device):
        return pltpu.make_async_remote_copy(
            src_ref=src,
            dst_ref=dst,
            send_sem=halo_send.at[k],
            recv_sem=halo_recv.at[k],
            device_id=device,
            device_id_type=MESH,
        )

    copies = [
        halo_copy(0, grids.at[:, head, :], from_down, (region, up)),
        halo_copy(1, grids.at[:, tail, :], from_up, (region, down)),
        halo_copy(2, edge.at[head, :], corner.at[0], (left, up)),
        halo_copy(3, edge.at[head, :], corner.at[1], (right, up)),
        halo_copy(4, edge.at[tail, :], corner.at[2], (left, down)),
        halo_copy(5, edge.at[tail, :], corner.at[3], (right, down)),
        halo_copy(6, edge_turned.at[pl.ds(0, 2 * HALO), :], from_side.at[0], (left, tile)),
        halo_copy(7, edge_turned.at[pl.ds(side - 2 * HALO, 2 * HALO), :], from_side.at[1], (right, tile)),
    ]
    for copy in copies[:2]:
        copy.start()
    density, heights = grids[0], grids[1]
    lane = iota((side, side), 1)
    both = jnp.where(
        (lane < HALO) | (lane >= last),
        density,
        jnp.where(lane < 2 * HALO, pltpu.roll(heights, HALO, 1), pltpu.roll(heights, last, 1)),
    )
    edge[...] = both
    for copy in copies[2:6]:
        copy.start()
    edge_turned[...] = both.T
    for copy in copies[6:]:
        copy.start()

    panels_side = side // PB
    all_panels = n_tile * panels_side
    reach_x = all_panels / 4.0
    reach_y = panels_side / 2.0
    own_row = iota((panels_side, all_panels), 0) + tile * panels_side
    slot = iota((panels_side, all_panels), 1)
    source = tile - slot // panels_side
    source = jnp.where(source < 0, source + n_tile, source)
    gap_x = (own_row - source * panels_side - slot % panels_side).astype(F32)
    kernel_x = jnp.exp(-(gap_x * gap_x) / (2.0 * reach_x * reach_x))
    gap_y = (iota((side, side), 0) // PB - iota((side, side), 1) // PB).astype(F32)
    area = 1.0 / (PB * PB)
    mean_of = jnp.where(gap_y == 0.0, area, 0.0)
    smooth_of = jnp.exp(-(gap_y * gap_y) / (2.0 * reach_y * reach_y)) * area
    sum_y = jnp.sum(smooth_of, axis=0, keepdims=True) * (1.0 * PB)
    inverse = 1.0 / (jnp.sum(kernel_x, axis=1, keepdims=True) * sum_y)

    rows_all = side + 2 * HALO
    cells[...] = jnp.zeros_like(cells)
    curved[...] = jnp.zeros_like(curved)
    row_at = iota((rows_all, side), 0) - HALO + tile * side
    lane_at = iota((rows_all, side), 1)
    row_inside = (row_at >= 0) & (row_at < n_tile * side)
    side_inside = ((lane_at < HALO) & (region < n_region - 1)) | ((lane_at >= last) & (region > 0))
    insides = (row_inside, row_inside & side_inside)
    strip = iota((HALO, side), 1)
    middle = jnp.zeros((side - 2 * HALO, side), F32)

    for copy in copies:
        copy.wait()

    for g, own in enumerate((density, heights)):
        field[g, 0, HALO : HALO + side, :] = own
        field[g, 0, 0:HALO, :] = from_up[g]
        field[g, 0, HALO + side : rows_all, :] = from_down[g]
        of_right = from_side[0, g * HALO : (g + 1) * HALO, :]
        of_left = from_side[1, (1 - g) * HALO : (2 - g) * HALO, :]
        field[g, 1, HALO : HALO + side, :] = jnp.concatenate([of_right, middle, of_left], axis=0).T
        for rows, pair in ((slice(0, HALO), (2, 3)), (slice(HALO + side, rows_all), (0, 1))):
            of_right, of_left = corner[pair[0]], corner[pair[1]]
            if g == 1:
                of_right, of_left = pltpu.roll(of_right, last, 1), pltpu.roll(of_left, HALO, 1)
            field[g, 1, rows, :] = jnp.where(
                strip < HALO, of_right, jnp.where(strip >= last, of_left, 0.0)
            )
    for k, inside in enumerate(insides):
        dens, hts = field[0, k], field[1, k]
        field[2, k] = jnp.where(inside, relaxation / (dens + 20.0 * stiffness), 0.0)
        cells[k, PAD : PAD + rows_all, :] = jnp.where(inside, hts / (dens + 1.0), 0.0)

    def sweep(_, carry):
        for first in range(0, rows_all, ROWS):
            bent = laplacian(cells, first)
            for k in range(2):
                curved[k, PAD + first : PAD + first + ROWS, :] = bent[k]
        for first in range(0, rows_all, ROWS):
            bent = laplacian(curved, first)
            rows = slice(first, first + ROWS)
            for k in range(2):
                v = cells[k, PAD + first : PAD + first + ROWS, :]
                residue = field[1, k, rows, :] - field[0, k, rows, :] * v - stiffness * bent[k]
                cells[k, PAD + first : PAD + first + ROWS, :] = v + field[2, k, rows, :] * residue
        return carry

    lax.fori_loop(0, SWEEPS, sweep, 0, unroll=SWEEPS)
    terrain = cells[0, PAD + HALO : PAD + HALO + side, :]
    terrain_ref[...] = terrain

    sums = jnp.sum(terrain.reshape(panels_side, PB, side), axis=1)
    smooth[...] = dot_exact(sums, smooth_of)

    def panel_copy(shift):
        return pltpu.make_async_remote_copy(
            src_ref=smooth,
            dst_ref=gathered.at[shift],
            send_sem=panel_send.at[shift],
            recv_sem=panel_recv.at[shift],
            device_id=(region, lax.rem(tile + shift, n_tile)),
            device_id_type=MESH,
        )

    def send_panel(place, carry):
        panel_copy(lax.rem(place + n_tile // 2 - 1, n_tile - 1) + 1).start()
        return carry

    lax.fori_loop(0, n_tile - 1, send_panel, 0)
    gathered[0] = smooth[...]
    panels = dot_exact(sums, mean_of)
    misfit = jnp.abs(grids[1] - grids[0] * terrain) / (grids[0] + 1.0)

    def wait_panel(shift, carry):
        panel_copy(shift).wait()
        return carry

    lax.fori_loop(1, n_tile, wait_panel, 0)
    numer = dot_exact(kernel_x, gathered[...].reshape(all_panels, side))
    limit = base_slack + slope_slack * jnp.abs(panels - numer * inverse)
    limit = jnp.broadcast_to(limit[:, None, :], (panels_side, PB, side)).reshape(side, side)
    limit = jnp.where(fixed_ref[...] == 1, base_slack, limit)
    soft_ref[...] = 1.0 / (1.0 + jnp.exp((misfit - limit) / softness))


def on_device(n_region, n_tile, pts_coords, pts_height, pts_weight, block_dest, block_count, ground_mask, fixed_mask):
    blocks, points = pts_height.shape
    side = fixed_mask.shape[0]
    rows_all = side + 2 * HALO
    panels_side = side // PB
    out = jax.ShapeDtypeStruct((side, side), F32)
    dma = pltpu.SemaphoreType.DMA
    return pl.pallas_call(
        functools.partial(kernel, n_region, n_tile),
        out_shape=(out, out),
        in_specs=[pl.BlockSpec(memory_space=pltpu.HBM)] * 7,
        out_specs=[pl.BlockSpec(memory_space=pltpu.VMEM)] * 2,
        scratch_shapes=[
            pltpu.VMEM((2, blocks, points), F32),
            pltpu.VMEM((blocks, points), F32),
            pltpu.VMEM((blocks, points), F32),
            pltpu.VMEM((1, blocks), jnp.int32),
            pltpu.VMEM((1, blocks), jnp.int32),
            pltpu.VMEM((blocks, points), jnp.int32),
            pltpu.VMEM((side, side), jnp.int32),
            pltpu.VMEM((3 * blocks, 4 * points), BF16),
            pltpu.VMEM((n_tile, 4 * CAP, points), F32),
            pltpu.VMEM((n_tile, 4 * CAP, points), F32),
            pltpu.VMEM((2, 2 * side, 4 * points), BF16),
            pltpu.VMEM((2, side, 4 * points), BF16),
            pltpu.VMEM((2, side, side), F32),
            pltpu.VMEM((side, side), F32),
            pltpu.VMEM((side, side), F32),
            pltpu.VMEM((2, HALO, side), F32),
            pltpu.VMEM((2, HALO, side), F32),
            pltpu.VMEM((2, 2 * HALO, side), F32),
            pltpu.VMEM((4, HALO, side), F32),
            pltpu.VMEM((3, 2, rows_all, side), F32),
            pltpu.VMEM((2, rows_all + 2 * PAD, side), F32),
            pltpu.VMEM((2, rows_all + 2 * PAD, side), F32),
            pltpu.VMEM((panels_side, side), F32),
            pltpu.VMEM((n_tile, panels_side, side), F32),
            dma((n_tile,)),
            dma((n_tile,)),
            dma((8,)),
            dma((8,)),
            dma((n_tile,)),
            dma((n_tile,)),
            dma((8,)),
        ],
        compiler_params=pltpu.CompilerParams(
            collective_id=0, has_side_effects=True, vmem_limit_bytes=40 << 20
        ),
    )(
        *[
            pltpu.with_memory_space_constraint(operand, pltpu.HBM)
            for operand in (
                pts_coords,
                pts_height,
                pts_weight,
                block_dest.reshape(1, blocks),
                block_count.reshape(1, blocks),
                ground_mask,
                fixed_mask,
            )
        ]
    )


def solution(mesh):
    placed = (
        P(("region", "tile"), None, None),
        P(("region", "tile"), None),
        P(("region", "tile"), None),
        P(("region", "tile"), None),
        P(("region", "tile")),
        P(("region", "tile"), None),
        P("tile", "region"),
    )
    return jax.shard_map(
        functools.partial(on_device, mesh.shape["region"], mesh.shape["tile"]),
        mesh=mesh,
        in_specs=placed,
        out_specs=(P("tile", "region"), P("tile", "region")),
        check_vma=False,
    )
```

```python
import functools

import jax
import jax.numpy as jnp
from jax import lax
from jax.experimental import pallas as pl
from jax.experimental.pallas import tpu as pltpu
from jax.sharding import PartitionSpec as P

MESH = pl.DeviceIdType.MESH
F32 = jnp.float32
BF16 = jnp.bfloat16

PB = 16
SWEEPS = 8
HALO = 2 * SWEEPS
CAP = 16
WINDOW = 18
GROUPS = 4
PAD = 8
ROWS = 32

stiffness = 1.0
relaxation = 0.5
base_slack = 0.3
slope_slack = 1.0
softness = 0.2


def iota(shape, dim):
    return lax.broadcasted_iota(jnp.int32, shape, dim)


def tent(coord, anchor):
    return jnp.maximum(0.0, 1.0 - jnp.abs(coord - anchor))


def partner_order(n_tile):
    if n_tile != 32:
        return list(range(n_tile))
    load = [0] * 5
    left = set(range(1, 32))
    order = [0]
    while left:

        def after(step):
            dx, dz, dy = step // 8, step // 4 % 2, step % 4
            added = (dx in (1, 2), dx in (2, 3), dy in (1, 2), dy in (2, 3), dz)
            return [have + more for have, more in zip(load, added)]

        step = min(left, key=lambda c: (sum(after(c)), max(after(c)), sum(v * v for v in after(c)), c))
        load = after(step)
        left.remove(step)
        order.append(step)
    return order


def tile_step(tile, k, n_tile):
    order = partner_order(n_tile)
    step = order[0]
    for place in range(1, n_tile):
        step = jnp.where(k == place, order[place], step)
    if n_tile != 32:
        return lax.rem(tile + step, n_tile)
    x, z, y = tile // 8, lax.rem(tile // 4, 2), lax.rem(tile, 4)
    x = lax.rem(x + step // 8, 4)
    z = lax.rem(z + step // 4, 2)
    y = lax.rem(y + step, 4)
    return (x * 2 + z) * 4 + y


def order_of(dest, tile, n_tile):
    if n_tile != 32:
        return (dest - tile + n_tile) & (n_tile - 1)
    dx = ((dest >> 3) - tile // 8) & 3
    dz = ((dest >> 2) - tile // 4) & 1
    dy = (dest - tile) & 3
    step = dx * 8 + dz * 4 + dy
    place = jnp.zeros_like(step)
    for at, candidate in enumerate(partner_order(n_tile)):
        place = jnp.where(step == candidate, at, place)
    return place


def dot_exact(a, b):
    return jnp.dot(a, b, precision=lax.Precision.HIGHEST, preferred_element_type=F32)


def laplacian(cells, first):
    side = cells.shape[2]
    lane = iota((ROWS, side), 1)
    centre = [cells[k, PAD + first : PAD + first + ROWS, :] for k in range(2)]
    after = [pltpu.roll(c, 1, 1) for c in centre]
    before = [pltpu.roll(c, side - 1, 1) for c in centre]
    out = []
    for k in range(2):
        west = jnp.where(lane == 0, after[1 - k], after[k])
        east = jnp.where(lane == side - 1, before[1 - k], before[k])
        north = cells[k, PAD + first - 1 : PAD + first - 1 + ROWS, :]
        south = cells[k, PAD + first + 1 : PAD + first + 1 + ROWS, :]
        out.append((west + east) + (north + south) - 4.0 * centre[k])
    return out


def kernel(
    n_region,
    n_tile,
    coords_hbm,
    height_hbm,
    weight_hbm,
    dest_hbm,
    count_hbm,
    ground_hbm,
    fixed_hbm,
    terrain_ref,
    soft_ref,
    coords_ref,
    height_ref,
    weight_ref,
    dest_ref,
    count_ref,
    ground_ref,
    fixed_ref,
    payload,
    outbox,
    inbox,
    left_buf,
    right_buf,
    grids,
    edge,
    edge_turned,
    from_up,
    from_down,
    from_side,
    corner,
    field,
    cells,
    curved,
    smooth,
    gathered,
    box_send,
    box_recv,
    halo_send,
    halo_recv,
    panel_send,
    panel_recv,
    load_sem,
):
    region = lax.axis_index("region")
    tile = lax.axis_index("tile")
    blocks, points = height_hbm.shape
    side = fixed_hbm.shape[0]
    right = lax.rem(region + 1, n_region)
    left = lax.rem(region + n_region - 1, n_region)
    down = lax.rem(tile + 1, n_tile)
    up = lax.rem(tile + n_tile - 1, n_tile)

    loads = [
        pltpu.make_async_copy(src, dst, load_sem.at[i])
        for i, (src, dst) in enumerate(
            (
                (dest_hbm, dest_ref),
                (count_hbm, count_ref),
                (ground_hbm, ground_ref),
                (weight_hbm, weight_ref),
                (height_hbm, height_ref),
                (coords_hbm.at[:, 0, :], coords_ref.at[0]),
                (coords_hbm.at[:, 1, :], coords_ref.at[1]),
                (fixed_hbm, fixed_ref),
            )
        )
    ]
    for load in loads:
        load.start()

    barrier = pltpu.get_barrier_semaphore()

    def greet(shift, carry):
        pl.semaphore_signal(
            barrier, inc=1, device_id=(region, lax.rem(tile + shift, n_tile)), device_id_type=MESH
        )
        return carry

    lax.fori_loop(1, n_tile, greet, 0)
    for other in (left, right):
        for row in (up, tile, down):
            pl.semaphore_signal(barrier, inc=1, device_id=(other, row), device_id_type=MESH)

    for load in loads[:2]:
        load.wait()
    eye = iota((blocks, blocks), 0) == iota((blocks, blocks), 1)
    dest_row = dest_ref[...].astype(F32)
    dest_col = jnp.sum(jnp.where(eye, dest_row, 0.0), axis=1, keepdims=True)
    count_col = jnp.sum(jnp.where(eye, count_ref[...].astype(F32), 0.0), axis=1, keepdims=True)
    earlier = iota((blocks, blocks), 0) < iota((blocks, blocks), 1)
    order = jnp.sum(jnp.where((dest_col == dest_row) & earlier, 1.0, 0.0), axis=0, keepdims=True)
    slot_row = order_of(dest_ref[...], tile, n_tile).astype(F32) * CAP + order

    def split(q, value):
        for part in range(3):
            rounded = value.astype(BF16)
            payload[part * blocks : (part + 1) * blocks, q * points : (q + 1) * points] = rounded
            value = value - rounded.astype(F32)

    for load in loads[2:4]:
        load.wait()
    live = (iota((blocks, points), 1).astype(F32) < count_col) & (ground_ref[...] == 1)
    weight = jnp.where(live, weight_ref[...], 0.0)
    split(2, weight)
    loads[4].wait()
    split(3, weight * height_ref[...])
    loads[5].wait()
    split(0, coords_ref[0])
    loads[6].wait()
    split(1, coords_ref[1])
    loads[7].wait()

    def box_copy(shift):
        return pltpu.make_async_remote_copy(
            src_ref=outbox.at[shift],
            dst_ref=inbox.at[shift],
            send_sem=box_send.at[shift],
            recv_sem=box_recv.at[shift],
            device_id=(region, tile_step(tile, shift, n_tile)),
            device_id_type=MESH,
        )

    window = min(WINDOW, n_tile - 1)
    group = n_tile // GROUPS
    for first in range(0, n_tile, group):
        slots = iota((group * CAP, blocks), 0) + first * CAP
        pick = jnp.where(slots.astype(F32) == slot_row, 1.0, 0.0).astype(BF16)
        pick = jnp.concatenate([pick] * 3, axis=1)
        for q in range(4):
            picked = jnp.dot(pick, payload[:, q * points : (q + 1) * points], preferred_element_type=F32)
            outbox[first : first + group, q * CAP : (q + 1) * CAP, :] = picked.reshape(group, CAP, points)
        if first == 0:
            pl.semaphore_wait(barrier, n_tile - 1 + 6)

        def send(shift, carry):
            box_copy(shift).start()
            return carry

        lax.fori_loop(max(first, 1), max(first, min(first + group, window + 1)), send, 0)

    inbox[0] = outbox[0]
    grids[...] = jnp.zeros_like(grids)
    anchors = iota((16, points), 0).astype(F32).astype(BF16)
    zero = jnp.zeros((16, points), BF16)

    def splat(shift, carry):
        @pl.when(shift > 0)
        def _():
            box_copy(shift).wait_send()

        @pl.when((shift > 0) & (shift + window < n_tile))
        def _():
            box_copy(shift + window).start()

        @pl.when(shift > 0)
        def _():
            box_copy(shift).wait_recv()

        box = inbox[shift]
        x, y, w, u = [box[q * CAP : (q + 1) * CAP, :] for q in range(4)]
        x_low, y_low = jnp.floor(x), jnp.floor(y)
        x_high, y_high = x_low + 1.0, y_low + 1.0
        tx0, tx1 = tent(x, x_low), tent(x, x_high)
        rows = (x_low, x_high, y_low, y_high, w * tx0, w * tx1, u * tx0, u * tx1, tent(y, y_low), tent(y, y_high))
        for j in range(CAP):
            slot, col = (j // 4) % 2, (j % 4) * points
            spread = [jnp.broadcast_to(r[j : j + 1, :], (16, points)).astype(BF16) for r in rows]
            xl, xh, yl, yh, w0, w1, u0, u1, r0, r1 = spread
            for t in range(side // 16):
                at = anchors + BF16(16 * t)
                low, high = at == xl, at == xh
                lanes = slice(col, col + points)
                left_buf[slot, 16 * t : 16 * t + 16, lanes] = jnp.where(low, w0, jnp.where(high, w1, zero))
                left_buf[slot, side + 16 * t : side + 16 * t + 16, lanes] = jnp.where(
                    low, u0, jnp.where(high, u1, zero)
                )
                right_buf[slot, 16 * t : 16 * t + 16, lanes] = jnp.where(
                    at == yl, r0, jnp.where(at == yh, r1, zero)
                )
            if j % 4 == 3:
                grids[...] += lax.dot_general(
                    left_buf[slot], right_buf[slot], (((1,), (1,)), ((), ())), preferred_element_type=F32
                ).reshape(2, side, side)
        return carry

    lax.fori_loop(0, n_tile, splat, 0)

    last = side - HALO
    head, tail = pl.ds(0, HALO), pl.ds(last, HALO)

    def halo_copy(k, src, dst, device):
        return pltpu.make_async_remote_copy(
            src_ref=src,
            dst_ref=dst,
            send_sem=halo_send.at[k],
            recv_sem=halo_recv.at[k],
            device_id=device,
            device_id_type=MESH,
        )

    copies = [
        halo_copy(0, grids.at[:, head, :], from_down, (region, up)),
        halo_copy(1, grids.at[:, tail, :], from_up, (region, down)),
        halo_copy(2, edge.at[head, :], corner.at[0], (left, up)),
        halo_copy(3, edge.at[head, :], corner.at[1], (right, up)),
        halo_copy(4, edge.at[tail, :], corner.at[2], (left, down)),
        halo_copy(5, edge.at[tail, :], corner.at[3], (right, down)),
        halo_copy(6, edge_turned.at[pl.ds(0, 2 * HALO), :], from_side.at[0], (left, tile)),
        halo_copy(7, edge_turned.at[pl.ds(side - 2 * HALO, 2 * HALO), :], from_side.at[1], (right, tile)),
    ]
    for copy in copies[:2]:
        copy.start()
    density, heights = grids[0], grids[1]
    lane = iota((side, side), 1)
    both = jnp.where(
        (lane < HALO) | (lane >= last),
        density,
        jnp.where(lane < 2 * HALO, pltpu.roll(heights, HALO, 1), pltpu.roll(heights, last, 1)),
    )
    edge[...] = both
    for copy in copies[2:6]:
        copy.start()
    edge_turned[...] = both.T
    for copy in copies[6:]:
        copy.start()

    panels_side = side // PB
    all_panels = n_tile * panels_side
    reach_x = all_panels / 4.0
    reach_y = panels_side / 2.0
    own_row = iota((panels_side, all_panels), 0) + tile * panels_side
    slot = iota((panels_side, all_panels), 1)
    source = tile - slot // panels_side
    source = jnp.where(source < 0, source + n_tile, source)
    gap_x = (own_row - source * panels_side - slot % panels_side).astype(F32)
    kernel_x = jnp.exp(-(gap_x * gap_x) / (2.0 * reach_x * reach_x))
    gap_y = (iota((side, side), 0) // PB - iota((side, side), 1) // PB).astype(F32)
    area = 1.0 / (PB * PB)
    mean_of = jnp.where(gap_y == 0.0, area, 0.0)
    smooth_of = jnp.exp(-(gap_y * gap_y) / (2.0 * reach_y * reach_y)) * area
    sum_y = jnp.sum(smooth_of, axis=0, keepdims=True) * (1.0 * PB)
    inverse = 1.0 / (jnp.sum(kernel_x, axis=1, keepdims=True) * sum_y)

    rows_all = side + 2 * HALO
    cells[...] = jnp.zeros_like(cells)
    curved[...] = jnp.zeros_like(curved)
    row_at = iota((rows_all, side), 0) - HALO + tile * side
    lane_at = iota((rows_all, side), 1)
    row_inside = (row_at >= 0) & (row_at < n_tile * side)
    side_inside = ((lane_at < HALO) & (region < n_region - 1)) | ((lane_at >= last) & (region > 0))
    insides = (row_inside, row_inside & side_inside)
    strip = iota((HALO, side), 1)
    middle = jnp.zeros((side - 2 * HALO, side), F32)

    for copy in copies:
        copy.wait()

    for g, own in enumerate((density, heights)):
        field[g, 0, HALO : HALO + side, :] = own
        field[g, 0, 0:HALO, :] = from_up[g]
        field[g, 0, HALO + side : rows_all, :] = from_down[g]
        of_right = from_side[0, g * HALO : (g + 1) * HALO, :]
        of_left = from_side[1, (1 - g) * HALO : (2 - g) * HALO, :]
        field[g, 1, HALO : HALO + side, :] = jnp.concatenate([of_right, middle, of_left], axis=0).T
        for rows, pair in ((slice(0, HALO), (2, 3)), (slice(HALO + side, rows_all), (0, 1))):
            of_right, of_left = corner[pair[0]], corner[pair[1]]
            if g == 1:
                of_right, of_left = pltpu.roll(of_right, last, 1), pltpu.roll(of_left, HALO, 1)
            field[g, 1, rows, :] = jnp.where(
                strip < HALO, of_right, jnp.where(strip >= last, of_left, 0.0)
            )
    for k, inside in enumerate(insides):
        dens, hts = field[0, k], field[1, k]
        field[2, k] = jnp.where(inside, relaxation / (dens + 20.0 * stiffness), 0.0)
        cells[k, PAD : PAD + rows_all, :] = jnp.where(inside, hts / (dens + 1.0), 0.0)

    def sweep(_, carry):
        for first in range(0, rows_all, ROWS):
            bent = laplacian(cells, first)
            for k in range(2):
                curved[k, PAD + first : PAD + first + ROWS, :] = bent[k]
        for first in range(0, rows_all, ROWS):
            bent = laplacian(curved, first)
            rows = slice(first, first + ROWS)
            for k in range(2):
                v = cells[k, PAD + first : PAD + first + ROWS, :]
                residue = field[1, k, rows, :] - field[0, k, rows, :] * v - stiffness * bent[k]
                cells[k, PAD + first : PAD + first + ROWS, :] = v + field[2, k, rows, :] * residue
        return carry

    lax.fori_loop(0, SWEEPS, sweep, 0, unroll=SWEEPS)
    terrain = cells[0, PAD + HALO : PAD + HALO + side, :]
    terrain_ref[...] = terrain

    sums = jnp.sum(terrain.reshape(panels_side, PB, side), axis=1)
    smooth[...] = dot_exact(sums, smooth_of)

    def panel_copy(shift):
        return pltpu.make_async_remote_copy(
            src_ref=smooth,
            dst_ref=gathered.at[shift],
            send_sem=panel_send.at[shift],
            recv_sem=panel_recv.at[shift],
            device_id=(region, lax.rem(tile + shift, n_tile)),
            device_id_type=MESH,
        )

    def send_panel(place, carry):
        panel_copy(lax.rem(place + n_tile // 2 - 1, n_tile - 1) + 1).start()
        return carry

    lax.fori_loop(0, n_tile - 1, send_panel, 0)
    gathered[0] = smooth[...]
    panels = dot_exact(sums, mean_of)
    misfit = jnp.abs(grids[1] - grids[0] * terrain) / (grids[0] + 1.0)

    def wait_panel(shift, carry):
        panel_copy(shift).wait()
        return carry

    lax.fori_loop(1, n_tile, wait_panel, 0)
    numer = dot_exact(kernel_x, gathered[...].reshape(all_panels, side))
    limit = base_slack + slope_slack * jnp.abs(panels - numer * inverse)
    limit = jnp.broadcast_to(limit[:, None, :], (panels_side, PB, side)).reshape(side, side)
    limit = jnp.where(fixed_ref[...] == 1, base_slack, limit)
    soft_ref[...] = 1.0 / (1.0 + jnp.exp((misfit - limit) / softness))


def on_device(n_region, n_tile, pts_coords, pts_height, pts_weight, block_dest, block_count, ground_mask, fixed_mask):
    blocks, points = pts_height.shape
    side = fixed_mask.shape[0]
    rows_all = side + 2 * HALO
    panels_side = side // PB
    out = jax.ShapeDtypeStruct((side, side), F32)
    dma = pltpu.SemaphoreType.DMA
    return pl.pallas_call(
        functools.partial(kernel, n_region, n_tile),
        out_shape=(out, out),
        in_specs=[pl.BlockSpec(memory_space=pltpu.HBM)] * 7,
        out_specs=[pl.BlockSpec(memory_space=pltpu.VMEM)] * 2,
        scratch_shapes=[
            pltpu.VMEM((2, blocks, points), F32),
            pltpu.VMEM((blocks, points), F32),
            pltpu.VMEM((blocks, points), F32),
            pltpu.VMEM((1, blocks), jnp.int32),
            pltpu.VMEM((1, blocks), jnp.int32),
            pltpu.VMEM((blocks, points), jnp.int32),
            pltpu.VMEM((side, side), jnp.int32),
            pltpu.VMEM((3 * blocks, 4 * points), BF16),
            pltpu.VMEM((n_tile, 4 * CAP, points), F32),
            pltpu.VMEM((n_tile, 4 * CAP, points), F32),
            pltpu.VMEM((2, 2 * side, 4 * points), BF16),
            pltpu.VMEM((2, side, 4 * points), BF16),
            pltpu.VMEM((2, side, side), F32),
            pltpu.VMEM((side, side), F32),
            pltpu.VMEM((side, side), F32),
            pltpu.VMEM((2, HALO, side), F32),
            pltpu.VMEM((2, HALO, side), F32),
            pltpu.VMEM((2, 2 * HALO, side), F32),
            pltpu.VMEM((4, HALO, side), F32),
            pltpu.VMEM((3, 2, rows_all, side), F32),
            pltpu.VMEM((2, rows_all + 2 * PAD, side), F32),
            pltpu.VMEM((2, rows_all + 2 * PAD, side), F32),
            pltpu.VMEM((panels_side, side), F32),
            pltpu.VMEM((n_tile, panels_side, side), F32),
            dma((n_tile,)),
            dma((n_tile,)),
            dma((8,)),
            dma((8,)),
            dma((n_tile,)),
            dma((n_tile,)),
            dma((8,)),
        ],
        compiler_params=pltpu.CompilerParams(
            collective_id=0, has_side_effects=True, vmem_limit_bytes=40 << 20
        ),
    )(
        *[
            pltpu.with_memory_space_constraint(operand, pltpu.HBM)
            for operand in (
                pts_coords,
                pts_height,
                pts_weight,
                block_dest.reshape(1, blocks),
                block_count.reshape(1, blocks),
                ground_mask,
                fixed_mask,
            )
        ]
    )


def solution(mesh):
    placed = (
        P(("region", "tile"), None, None),
        P(("region", "tile"), None),
        P(("region", "tile"), None),
        P(("region", "tile"), None),
        P(("region", "tile")),
        P(("region", "tile"), None),
        P("tile", "region"),
    )
    return jax.shard_map(
        functools.partial(on_device, mesh.shape["region"], mesh.shape["tile"]),
        mesh=mesh,
        in_specs=placed,
        out_specs=(P("tile", "region"), P("tile", "region")),
        check_vma=False,
    )
```

```python
import functools

import jax
import jax.numpy as jnp
from jax import lax
from jax.experimental import pallas as pl
from jax.experimental.pallas import tpu as pltpu
from jax.sharding import PartitionSpec as P

MESH = pl.DeviceIdType.MESH
F32 = jnp.float32
BF16 = jnp.bfloat16

PB = 16
SWEEPS = 8
HALO = 2 * SWEEPS
CAP = 16
WINDOW = 18
GROUPS = 4
PAD = 8
ROWS = 32

stiffness = 1.0
relaxation = 0.5
base_slack = 0.3
slope_slack = 1.0
softness = 0.2


def iota(shape, dim):
    return lax.broadcasted_iota(jnp.int32, shape, dim)


def tent(coord, anchor):
    return jnp.maximum(0.0, 1.0 - jnp.abs(coord - anchor))


def partner_order(n_tile):
    if n_tile != 32:
        return list(range(n_tile))
    load = [0] * 5
    left = set(range(1, 32))
    order = [0]
    while left:

        def after(step):
            dx, dz, dy = step // 8, step // 4 % 2, step % 4
            added = (dx in (1, 2), dx in (2, 3), dy in (1, 2), dy in (2, 3), dz)
            return [have + more for have, more in zip(load, added)]

        step = min(left, key=lambda c: (max(after(c)), sum(after(c)), sum(v * v for v in after(c)), c))
        load = after(step)
        left.remove(step)
        order.append(step)
    return order


def tile_step(tile, k, n_tile):
    order = partner_order(n_tile)
    if n_tile != 32:
        return lax.rem(tile + k, n_tile)
    words = [sum(order[4 * w + i] << (5 * i) for i in range(4)) for w in range(8)]
    high, low = k // 4, lax.rem(k, 4)
    word = words[0]
    for w in range(1, 8):
        word = jnp.where(high == w, words[w], word)
    step = word & 31
    for i in range(1, 4):
        step = jnp.where(low == i, (word >> (5 * i)) & 31, step)
    x, z, y = tile // 8, lax.rem(tile // 4, 2), lax.rem(tile, 4)
    x = lax.rem(x + step // 8, 4)
    z = lax.rem(z + step // 4, 2)
    y = lax.rem(y + step, 4)
    return (x * 2 + z) * 4 + y


def order_of(dest, tile, n_tile):
    if n_tile != 32:
        return (dest - tile + n_tile) & (n_tile - 1)
    dx = ((dest >> 3) - tile // 8) & 3
    dz = ((dest >> 2) - tile // 4) & 1
    dy = (dest - tile) & 3
    step = dx * 8 + dz * 4 + dy
    place = jnp.zeros_like(step)
    for at, candidate in enumerate(partner_order(n_tile)):
        place = jnp.where(step == candidate, at, place)
    return place


def dot_exact(a, b):
    return jnp.dot(a, b, precision=lax.Precision.HIGHEST, preferred_element_type=F32)


def laplacian(cells, first):
    side = cells.shape[2]
    lane = iota((ROWS, side), 1)
    centre = [cells[k, PAD + first : PAD + first + ROWS, :] for k in range(2)]
    after = [pltpu.roll(c, 1, 1) for c in centre]
    before = [pltpu.roll(c, side - 1, 1) for c in centre]
    out = []
    for k in range(2):
        west = jnp.where(lane == 0, after[1 - k], after[k])
        east = jnp.where(lane == side - 1, before[1 - k], before[k])
        north = cells[k, PAD + first - 1 : PAD + first - 1 + ROWS, :]
        south = cells[k, PAD + first + 1 : PAD + first + 1 + ROWS, :]
        out.append((west + east) + (north + south) - 4.0 * centre[k])
    return out


def kernel(
    n_region,
    n_tile,
    coords_hbm,
    height_hbm,
    weight_hbm,
    dest_hbm,
    count_hbm,
    ground_hbm,
    fixed_hbm,
    terrain_ref,
    soft_ref,
    coords_ref,
    height_ref,
    weight_ref,
    dest_ref,
    count_ref,
    ground_ref,
    fixed_ref,
    payload,
    outbox,
    inbox,
    left_buf,
    right_buf,
    grids,
    edge,
    edge_turned,
    from_up,
    from_down,
    from_side,
    corner,
    field,
    cells,
    curved,
    smooth,
    gathered,
    box_send,
    box_recv,
    halo_send,
    halo_recv,
    panel_send,
    panel_recv,
    load_sem,
):
    region = lax.axis_index("region")
    tile = lax.axis_index("tile")
    blocks, points = height_hbm.shape
    side = fixed_hbm.shape[0]
    right = lax.rem(region + 1, n_region)
    left = lax.rem(region + n_region - 1, n_region)
    down = lax.rem(tile + 1, n_tile)
    up = lax.rem(tile + n_tile - 1, n_tile)

    loads = [
        pltpu.make_async_copy(src, dst, load_sem.at[i])
        for i, (src, dst) in enumerate(
            (
                (dest_hbm, dest_ref),
                (count_hbm, count_ref),
                (ground_hbm, ground_ref),
                (weight_hbm, weight_ref),
                (height_hbm, height_ref),
                (coords_hbm.at[:, 0, :], coords_ref.at[0]),
                (coords_hbm.at[:, 1, :], coords_ref.at[1]),
                (fixed_hbm, fixed_ref),
            )
        )
    ]
    for load in loads:
        load.start()

    barrier = pltpu.get_barrier_semaphore()

    def greet(shift, carry):
        pl.semaphore_signal(
            barrier, inc=1, device_id=(region, lax.rem(tile + shift, n_tile)), device_id_type=MESH
        )
        return carry

    lax.fori_loop(1, n_tile, greet, 0)
    for other in (left, right):
        for row in (up, tile, down):
            pl.semaphore_signal(barrier, inc=1, device_id=(other, row), device_id_type=MESH)

    for load in loads[:2]:
        load.wait()
    eye = iota((blocks, blocks), 0) == iota((blocks, blocks), 1)
    dest_row = dest_ref[...].astype(F32)
    dest_col = jnp.sum(jnp.where(eye, dest_row, 0.0), axis=1, keepdims=True)
    count_col = jnp.sum(jnp.where(eye, count_ref[...].astype(F32), 0.0), axis=1, keepdims=True)
    earlier = iota((blocks, blocks), 0) < iota((blocks, blocks), 1)
    order = jnp.sum(jnp.where((dest_col == dest_row) & earlier, 1.0, 0.0), axis=0, keepdims=True)
    slot_row = order_of(dest_ref[...], tile, n_tile).astype(F32) * CAP + order

    def split(q, value):
        for part in range(3):
            rounded = value.astype(BF16)
            payload[part * blocks : (part + 1) * blocks, q * points : (q + 1) * points] = rounded
            value = value - rounded.astype(F32)

    for load in loads[2:4]:
        load.wait()
    live = (iota((blocks, points), 1).astype(F32) < count_col) & (ground_ref[...] == 1)
    weight = jnp.where(live, weight_ref[...], 0.0)
    split(2, weight)
    loads[4].wait()
    split(3, weight * height_ref[...])
    loads[5].wait()
    split(0, coords_ref[0])
    loads[6].wait()
    split(1, coords_ref[1])
    loads[7].wait()

    def box_copy(shift):
        return pltpu.make_async_remote_copy(
            src_ref=outbox.at[shift],
            dst_ref=inbox.at[shift],
            send_sem=box_send.at[shift],
            recv_sem=box_recv.at[shift],
            device_id=(region, tile_step(tile, shift, n_tile)),
            device_id_type=MESH,
        )

    window = min(WINDOW, n_tile - 1)
    group = n_tile // GROUPS
    for first in range(0, n_tile, group):
        slots = iota((group * CAP, blocks), 0) + first * CAP
        pick = jnp.where(slots.astype(F32) == slot_row, 1.0, 0.0).astype(BF16)
        pick = jnp.concatenate([pick] * 3, axis=1)
        for q in range(4):
            picked = jnp.dot(pick, payload[:, q * points : (q + 1) * points], preferred_element_type=F32)
            outbox[first : first + group, q * CAP : (q + 1) * CAP, :] = picked.reshape(group, CAP, points)
        if first == 0:
            pl.semaphore_wait(barrier, n_tile - 1 + 6)

        def send(shift, carry):
            box_copy(shift).start()
            return carry

        lax.fori_loop(max(first, 1), max(first, min(first + group, window + 1)), send, 0)

    inbox[0] = outbox[0]
    grids[...] = jnp.zeros_like(grids)
    anchors = iota((16, points), 0).astype(F32).astype(BF16)
    zero = jnp.zeros((16, points), BF16)

    def splat(shift, carry):
        @pl.when(shift > 0)
        def _():
            box_copy(shift).wait_send()

        @pl.when((shift > 0) & (shift + window < n_tile))
        def _():
            box_copy(shift + window).start()

        @pl.when(shift > 0)
        def _():
            box_copy(shift).wait_recv()

        box = inbox[shift]
        x, y, w, u = [box[q * CAP : (q + 1) * CAP, :] for q in range(4)]
        x_low, y_low = jnp.floor(x), jnp.floor(y)
        x_high, y_high = x_low + 1.0, y_low + 1.0
        tx0, tx1 = tent(x, x_low), tent(x, x_high)
        rows = (x_low, x_high, y_low, y_high, w * tx0, w * tx1, u * tx0, u * tx1, tent(y, y_low), tent(y, y_high))
        for j in range(CAP):
            slot, col = (j // 4) % 2, (j % 4) * points
            spread = [jnp.broadcast_to(r[j : j + 1, :], (16, points)).astype(BF16) for r in rows]
            xl, xh, yl, yh, w0, w1, u0, u1, r0, r1 = spread
            for t in range(side // 16):
                at = anchors + BF16(16 * t)
                low, high = at == xl, at == xh
                lanes = slice(col, col + points)
                left_buf[slot, 16 * t : 16 * t + 16, lanes] = jnp.where(low, w0, jnp.where(high, w1, zero))
                left_buf[slot, side + 16 * t : side + 16 * t + 16, lanes] = jnp.where(
                    low, u0, jnp.where(high, u1, zero)
                )
                right_buf[slot, 16 * t : 16 * t + 16, lanes] = jnp.where(
                    at == yl, r0, jnp.where(at == yh, r1, zero)
                )
            if j % 4 == 3:
                grids[...] += lax.dot_general(
                    left_buf[slot], right_buf[slot], (((1,), (1,)), ((), ())), preferred_element_type=F32
                ).reshape(2, side, side)
        return carry

    lax.fori_loop(0, n_tile, splat, 0)

    last = side - HALO
    head, tail = pl.ds(0, HALO), pl.ds(last, HALO)

    def halo_copy(k, src, dst, device):
        return pltpu.make_async_remote_copy(
            src_ref=src,
            dst_ref=dst,
            send_sem=halo_send.at[k],
            recv_sem=halo_recv.at[k],
            device_id=device,
            device_id_type=MESH,
        )

    copies = [
        halo_copy(0, grids.at[:, head, :], from_down, (region, up)),
        halo_copy(1, grids.at[:, tail, :], from_up, (region, down)),
        halo_copy(2, edge.at[head, :], corner.at[0], (left, up)),
        halo_copy(3, edge.at[head, :], corner.at[1], (right, up)),
        halo_copy(4, edge.at[tail, :], corner.at[2], (left, down)),
        halo_copy(5, edge.at[tail, :], corner.at[3], (right, down)),
        halo_copy(6, edge_turned.at[pl.ds(0, 2 * HALO), :], from_side.at[0], (left, tile)),
        halo_copy(7, edge_turned.at[pl.ds(side - 2 * HALO, 2 * HALO), :], from_side.at[1], (right, tile)),
    ]
    for copy in copies[:2]:
        copy.start()
    density, heights = grids[0], grids[1]
    lane = iota((side, side), 1)
    both = jnp.where(
        (lane < HALO) | (lane >= last),
        density,
        jnp.where(lane < 2 * HALO, pltpu.roll(heights, HALO, 1), pltpu.roll(heights, last, 1)),
    )
    edge[...] = both
    for copy in copies[2:6]:
        copy.start()
    edge_turned[...] = both.T
    for copy in copies[6:]:
        copy.start()

    panels_side = side // PB
    all_panels = n_tile * panels_side
    reach_x = all_panels / 4.0
    reach_y = panels_side / 2.0
    own_row = iota((panels_side, all_panels), 0) + tile * panels_side
    slot = iota((panels_side, all_panels), 1)
    source = tile - slot // panels_side
    source = jnp.where(source < 0, source + n_tile, source)
    gap_x = (own_row - source * panels_side - slot % panels_side).astype(F32)
    kernel_x = jnp.exp(-(gap_x * gap_x) / (2.0 * reach_x * reach_x))
    gap_y = (iota((side, side), 0) // PB - iota((side, side), 1) // PB).astype(F32)
    area = 1.0 / (PB * PB)
    mean_of = jnp.where(gap_y == 0.0, area, 0.0)
    smooth_of = jnp.exp(-(gap_y * gap_y) / (2.0 * reach_y * reach_y)) * area
    sum_y = jnp.sum(smooth_of, axis=0, keepdims=True) * (1.0 * PB)
    inverse = 1.0 / (jnp.sum(kernel_x, axis=1, keepdims=True) * sum_y)

    rows_all = side + 2 * HALO
    cells[...] = jnp.zeros_like(cells)
    curved[...] = jnp.zeros_like(curved)
    row_at = iota((rows_all, side), 0) - HALO + tile * side
    lane_at = iota((rows_all, side), 1)
    row_inside = (row_at >= 0) & (row_at < n_tile * side)
    side_inside = ((lane_at < HALO) & (region < n_region - 1)) | ((lane_at >= last) & (region > 0))
    insides = (row_inside, row_inside & side_inside)
    strip = iota((HALO, side), 1)
    middle = jnp.zeros((side - 2 * HALO, side), F32)

    for copy in copies:
        copy.wait()

    for g, own in enumerate((density, heights)):
        field[g, 0, HALO : HALO + side, :] = own
        field[g, 0, 0:HALO, :] = from_up[g]
        field[g, 0, HALO + side : rows_all, :] = from_down[g]
        of_right = from_side[0, g * HALO : (g + 1) * HALO, :]
        of_left = from_side[1, (1 - g) * HALO : (2 - g) * HALO, :]
        field[g, 1, HALO : HALO + side, :] = jnp.concatenate([of_right, middle, of_left], axis=0).T
        for rows, pair in ((slice(0, HALO), (2, 3)), (slice(HALO + side, rows_all), (0, 1))):
            of_right, of_left = corner[pair[0]], corner[pair[1]]
            if g == 1:
                of_right, of_left = pltpu.roll(of_right, last, 1), pltpu.roll(of_left, HALO, 1)
            field[g, 1, rows, :] = jnp.where(
                strip < HALO, of_right, jnp.where(strip >= last, of_left, 0.0)
            )
    for k, inside in enumerate(insides):
        dens, hts = field[0, k], field[1, k]
        field[2, k] = jnp.where(inside, relaxation / (dens + 20.0 * stiffness), 0.0)
        cells[k, PAD : PAD + rows_all, :] = jnp.where(inside, hts / (dens + 1.0), 0.0)

    def sweep(_, carry):
        for first in range(0, rows_all, ROWS):
            bent = laplacian(cells, first)
            for k in range(2):
                curved[k, PAD + first : PAD + first + ROWS, :] = bent[k]
        for first in range(0, rows_all, ROWS):
            bent = laplacian(curved, first)
            rows = slice(first, first + ROWS)
            for k in range(2):
                v = cells[k, PAD + first : PAD + first + ROWS, :]
                residue = field[1, k, rows, :] - field[0, k, rows, :] * v - stiffness * bent[k]
                cells[k, PAD + first : PAD + first + ROWS, :] = v + field[2, k, rows, :] * residue
        return carry

    lax.fori_loop(0, SWEEPS, sweep, 0, unroll=SWEEPS)
    terrain = cells[0, PAD + HALO : PAD + HALO + side, :]
    terrain_ref[...] = terrain

    sums = jnp.sum(terrain.reshape(panels_side, PB, side), axis=1)
    smooth[...] = dot_exact(sums, smooth_of)

    def panel_copy(shift):
        return pltpu.make_async_remote_copy(
            src_ref=smooth,
            dst_ref=gathered.at[shift],
            send_sem=panel_send.at[shift],
            recv_sem=panel_recv.at[shift],
            device_id=(region, lax.rem(tile + shift, n_tile)),
            device_id_type=MESH,
        )

    def send_panel(place, carry):
        panel_copy(lax.rem(place + n_tile // 2 - 1, n_tile - 1) + 1).start()
        return carry

    lax.fori_loop(0, n_tile - 1, send_panel, 0)
    gathered[0] = smooth[...]
    panels = dot_exact(sums, mean_of)
    misfit = jnp.abs(grids[1] - grids[0] * terrain) / (grids[0] + 1.0)

    def wait_panel(shift, carry):
        panel_copy(shift).wait()
        return carry

    lax.fori_loop(1, n_tile, wait_panel, 0)
    numer = dot_exact(kernel_x, gathered[...].reshape(all_panels, side))
    limit = base_slack + slope_slack * jnp.abs(panels - numer * inverse)
    limit = jnp.broadcast_to(limit[:, None, :], (panels_side, PB, side)).reshape(side, side)
    limit = jnp.where(fixed_ref[...] == 1, base_slack, limit)
    soft_ref[...] = 1.0 / (1.0 + jnp.exp((misfit - limit) / softness))


def on_device(n_region, n_tile, pts_coords, pts_height, pts_weight, block_dest, block_count, ground_mask, fixed_mask):
    blocks, points = pts_height.shape
    side = fixed_mask.shape[0]
    rows_all = side + 2 * HALO
    panels_side = side // PB
    out = jax.ShapeDtypeStruct((side, side), F32)
    dma = pltpu.SemaphoreType.DMA
    return pl.pallas_call(
        functools.partial(kernel, n_region, n_tile),
        out_shape=(out, out),
        in_specs=[pl.BlockSpec(memory_space=pltpu.HBM)] * 7,
        out_specs=[pl.BlockSpec(memory_space=pltpu.VMEM)] * 2,
        scratch_shapes=[
            pltpu.VMEM((2, blocks, points), F32),
            pltpu.VMEM((blocks, points), F32),
            pltpu.VMEM((blocks, points), F32),
            pltpu.VMEM((1, blocks), jnp.int32),
            pltpu.VMEM((1, blocks), jnp.int32),
            pltpu.VMEM((blocks, points), jnp.int32),
            pltpu.VMEM((side, side), jnp.int32),
            pltpu.VMEM((3 * blocks, 4 * points), BF16),
            pltpu.VMEM((n_tile, 4 * CAP, points), F32),
            pltpu.VMEM((n_tile, 4 * CAP, points), F32),
            pltpu.VMEM((2, 2 * side, 4 * points), BF16),
            pltpu.VMEM((2, side, 4 * points), BF16),
            pltpu.VMEM((2, side, side), F32),
            pltpu.VMEM((side, side), F32),
            pltpu.VMEM((side, side), F32),
            pltpu.VMEM((2, HALO, side), F32),
            pltpu.VMEM((2, HALO, side), F32),
            pltpu.VMEM((2, 2 * HALO, side), F32),
            pltpu.VMEM((4, HALO, side), F32),
            pltpu.VMEM((3, 2, rows_all, side), F32),
            pltpu.VMEM((2, rows_all + 2 * PAD, side), F32),
            pltpu.VMEM((2, rows_all + 2 * PAD, side), F32),
            pltpu.VMEM((panels_side, side), F32),
            pltpu.VMEM((n_tile, panels_side, side), F32),
            dma((n_tile,)),
            dma((n_tile,)),
            dma((8,)),
            dma((8,)),
            dma((n_tile,)),
            dma((n_tile,)),
            dma((8,)),
        ],
        compiler_params=pltpu.CompilerParams(
            collective_id=0, has_side_effects=True, vmem_limit_bytes=40 << 20
        ),
    )(
        *[
            pltpu.with_memory_space_constraint(operand, pltpu.HBM)
            for operand in (
                pts_coords,
                pts_height,
                pts_weight,
                block_dest.reshape(1, blocks),
                block_count.reshape(1, blocks),
                ground_mask,
                fixed_mask,
            )
        ]
    )


def solution(mesh):
    placed = (
        P(("region", "tile"), None, None),
        P(("region", "tile"), None),
        P(("region", "tile"), None),
        P(("region", "tile"), None),
        P(("region", "tile")),
        P(("region", "tile"), None),
        P("tile", "region"),
    )
    return jax.shard_map(
        functools.partial(on_device, mesh.shape["region"], mesh.shape["tile"]),
        mesh=mesh,
        in_specs=placed,
        out_specs=(P("tile", "region"), P("tile", "region")),
        check_vma=False,
    )
```
